32 devices in a mesh: dp: 8 (over y, x, core), ctx: 4 (over z).
Axes of the slice: x: 2, y: 2, z: 4, core: 2. Of those that a mesh axis runs over, the one named last changes fastest.
Arguments:
- roll_query: bfloat16 [8, 512, 4096], P('dp', 'ctx'), may hold values from -12 to 12
- roll_keys: bfloat16 [8, 512, 512], P('dp', 'ctx'), may hold values from -12 to 12
- roll_values: bfloat16 [8, 512, 512], P('dp', 'ctx'), may hold values from -6 to 6
- pack_dest: int32 [8, 64], P(None, 'ctx'), may hold values from 0 to 7, as said below
- segment_ids: int32 [8, 512], P('dp', 'ctx'), may hold values from 0 to 15, never falling along the last dimension, each value on 1 to 256 neighbouring positions
- reward_bins: int32 [8, 16], P('dp'), may hold values from 0 to 511
- reward_weight: float32 [4096], replicated, may hold values from -0.5 to 0.5
Outputs:
- attention_out: bfloat16 [8, 512, 4096], P('dp', 'ctx')
- reward_hist: float32 [512], replicated
The draws below stay inside these ranges and needn't reach their ends.
Inputs may be any that keep to these rules, and one draw needn't show every extreme that they name: For every column j the entries pack_dest[s, j] over s are a permutation of the packed sequences. Among the 16 columns of one ctx shard, at most 2 blocks go from one source to one packed sequence, and exactly 2 for some pair in every shard.
All inputs are finite; a program needn't handle non-finite values.
Results may differ from the reference program's by a relative error of at most 0.004.
Values may be sent and summed in bfloat16 or wider, within the bound.
No kernel may reach another device: no remote copies, remote signals or barrier semaphores. Data moves between devices by JAX's collectives and lax.ppermute only.
A program may use at most 64 MiB of HBM per device.

```python
import math
import jax
import jax.numpy as jnp
import numpy as np
from jax import lax

HQ = 32
HK = 4
HD = 128
TQ = 128
BLK = 8
SEGS = 16
BINS = 512
NB = 16
SEQ_LEN = 512
SEQS = 8


def draw_roll_query(key, part):
    full_shape = (SEQS, SEQ_LEN, HQ * HD)
    values = jnp.clip(jax.random.normal(jax.random.fold_in(key, 7), full_shape, jnp.float32), -4.0, 4.0)
    return values.astype(jnp.bfloat16)


def draw_roll_keys(key, part):
    full_shape = (SEQS, SEQ_LEN, HK * HD)
    values = jnp.clip(jax.random.normal(jax.random.fold_in(key, 19), full_shape, jnp.float32), -4.0, 4.0)
    return values.astype(jnp.bfloat16)


def draw_pack_dest(key, part):
    ctx_count = SEQ_LEN // TQ
    cycle_len = min(NB, SEQS)

    def one_shard(shard_key):
        split_keys = jax.random.split(shard_key, 5)
        relabel = jax.random.permutation(split_keys[0], SEQS).astype(jnp.int32)
        start_map = jax.random.permutation(split_keys[1], SEQS).astype(jnp.int32)
        distinct = jax.random.permutation(split_keys[3], SEQS).astype(jnp.int32)
        block_ids = jnp.arange(NB, dtype=jnp.int32)
        picked = block_ids % cycle_len
        offsets = distinct[picked]
        offsets = offsets[jax.random.permutation(split_keys[4], NB)]
        return relabel[(start_map[:, None] + offsets[None, :]) % SEQS]
    shard_keys = jax.random.split(jax.random.fold_in(key, 29), ctx_count)
    tables = jax.vmap(one_shard)(shard_keys)
    return jnp.transpose(tables, (1, 0, 2)).reshape(SEQS, ctx_count * NB).astype(jnp.int32)


def with_ends(result, rng, low, top_value):
    place = [jax.random.randint(jax.random.fold_in(rng, axis), (), 0, length) for axis, length in enumerate(result.shape)]
    longest = result.shape.index(max(result.shape))
    neighbour = place[:longest] + [(place[longest] + 1) % result.shape[longest]] + place[longest + 1:]
    return result.at[tuple(place)].set(low).at[tuple(neighbour)].set(top_value)


def level_of(rng, dims, cuts, low, largest):
    gain, own = 1.0, jax.random.fold_in(rng, 6)
    for position, shards_of in cuts:
        steps = jnp.exp(jax.random.uniform(jax.random.fold_in(own, position), (shards_of,), jnp.float32, low / len(cuts), largest / len(cuts)))
        gain = gain * jnp.repeat(steps, dims[position] // shards_of).reshape([-1 if axis == position else 1 for axis in range(len(dims))])
    return gain


def split_up(count, total, limit, lean):
    portions = [(1 << 20) // math.isqrt(grade ** lean) + 1 for grade in range(2, count + 1)]
    rest, given = total - limit - (count - 1), [1] * (count - 1)
    while rest > 0:
        candidates = [i for i in range(count - 1) if given[i] < limit]
        whole, remaining = sum([portions[i] for i in candidates]), rest
        for i in candidates:
            extra = min(limit - given[i], max(1, remaining * portions[i] // whole), rest)
            given[i] = given[i] + extra
            rest = rest - extra
    return np.array([limit] + given)


def uneven_parts(own_key, count, total, reach, skew):
    if count == 2:
        one = jax.random.randint(own_key, (), max(1, total - reach), min(reach, total - 1) + 1)
        return jnp.stack([one, total - one])
    lengths = jnp.asarray(split_up(count, total, reach, skew), jnp.int32)
    twos = (count - 1) // 2
    giver, receiver = lengths[1:1 + 2 * twos:2], lengths[2:2 + 2 * twos:2]
    margin = jnp.minimum(giver - 1, reach - receiver)
    passed = jax.random.randint(jax.random.fold_in(own_key, 1), (twos,), 0, 1 << 20) % (margin + 1)
    lengths = lengths.at[1:1 + 2 * twos:2].set(giver - passed).at[2:2 + 2 * twos:2].set(receiver + passed)
    return lengths[jax.random.permutation(jax.random.fold_in(own_key, 2), count)]


def normal_values(stream_key, dims, width, bound, pieces=(), kind=jnp.bfloat16):
    entries = jax.random.normal(stream_key, dims, jnp.float32) * width
    if len(pieces) > 0:
        entries = level_of(stream_key, dims, pieces, -0.22, 0.18) * entries
    return jnp.clip(entries, min=-bound, max=bound).astype(kind)


def setup_inputs(seed: int = 0) -> dict:
    keys = jax.random.split(jax.random.key(seed), 8)
    roll_query = draw_roll_query(jax.random.fold_in(keys[7], 71), 0)
    roll_keys = draw_roll_keys(jax.random.fold_in(keys[7], 71), 0)
    roll_values = normal_values(keys[2], (SEQS, SEQ_LEN, HK * HD), 1.0, 6.0, ((0, 8), (1, 4)))
    pack_dest = draw_pack_dest(jax.random.fold_in(keys[7], 71), 0)
    segment_ids = jax.vmap(lambda own: jnp.searchsorted(jnp.cumsum(uneven_parts(own, SEGS, SEQ_LEN, SEQ_LEN // 2, 2)), jnp.arange(SEQ_LEN), side="right"))(jax.random.split(keys[4], SEQS)).reshape((SEQS, SEQ_LEN)).astype(jnp.int32)
    reward_bins = with_ends(jax.random.randint(keys[5], (SEQS, SEGS), 0, BINS), jax.random.fold_in(keys[5], 1), 0, BINS - 1).astype(jnp.int32)
    reward_weight = normal_values(keys[6], (HQ * HD,), HD ** -0.5, 0.5, (), jnp.float32)
    return dict(roll_query=roll_query, roll_keys=roll_keys, roll_values=roll_values, pack_dest=pack_dest, segment_ids=segment_ids, reward_bins=reward_bins, reward_weight=reward_weight)


NEG = -1e+30

def attend_sequence(query_rows, key_rows, value_rows, segments):
    seq_total = query_rows.shape[0]
    group_size = HQ // HK
    score_scale = 1.0 / math.sqrt(HD)
    positions = jnp.arange(seq_total, dtype=jnp.int32)
    allowed = (segments[:, None] == segments[None, :]) & (positions[None, :] <= positions[:, None])
    query_heads = query_rows.reshape(seq_total, HK, group_size, HD)
    key_heads = key_rows.reshape(seq_total, HK, HD)
    value_heads = value_rows.reshape(seq_total, HK, HD)

    def one_group(head_index):
        queries = jnp.take(query_heads, head_index, axis=1).astype(jnp.float32)
        keys_one = jnp.take(key_heads, head_index, axis=1).astype(jnp.float32)
        values_one = jnp.take(value_heads, head_index, axis=1).astype(jnp.float32)
        scores = jnp.einsum('qjd,kd->jqk', queries, keys_one, precision=lax.Precision.HIGHEST) * score_scale
        scores = jnp.where(allowed[None], scores, NEG)
        row_top = lax.optimization_barrier(jnp.max(scores, axis=-1))
        weights = jnp.where(allowed[None], jnp.exp(scores - row_top[..., None]), 0.0)
        row_total = lax.optimization_barrier(jnp.sum(weights, axis=-1))
        rounded = lax.optimization_barrier(weights.astype(jnp.bfloat16)).astype(jnp.float32)
        mixed_rows = jnp.einsum('jqk,kd->qjd', rounded, values_one, precision=lax.Precision.HIGHEST)
        return mixed_rows / jnp.transpose(row_total)[..., None]
    per_group = lax.map(one_group, jnp.arange(HK, dtype=jnp.int32))
    return jnp.transpose(per_group, (1, 0, 2, 3)).reshape(seq_total, HQ * HD).astype(jnp.bfloat16)

def reference(roll_query, roll_keys, roll_values, pack_dest, segment_ids, reward_bins, reward_weight):
    column_count = pack_dest.shape[1]
    seq_total = roll_query.shape[1]
    source_ids = jnp.arange(SEQS, dtype=jnp.int32)
    matches = pack_dest[:, None, :] == source_ids[None, :, None]
    source_of = lax.optimization_barrier(jnp.sum(jnp.where(matches, source_ids[:, None, None], 0), axis=0)).astype(jnp.int32)
    columns = jnp.arange(column_count, dtype=jnp.int32)
    query_blocks = roll_query.reshape(SEQS, column_count, BLK, HQ * HD)
    key_blocks = roll_keys.reshape(SEQS, column_count, BLK, HK * HD)
    value_blocks = roll_values.reshape(SEQS, column_count, BLK, HK * HD)

    def one_sequence(seq_index):
        sources = source_of[seq_index]
        packed_query = query_blocks[sources, columns].reshape(seq_total, HQ * HD)
        packed_keys = key_blocks[sources, columns].reshape(seq_total, HK * HD)
        packed_values = value_blocks[sources, columns].reshape(seq_total, HK * HD)
        segments = segment_ids[seq_index]
        attended = attend_sequence(packed_query, packed_keys, packed_values, segments)
        next_seg = jnp.concatenate([segments[1:], jnp.full((1,), -1, jnp.int32)])
        is_end = segments != next_seg
        row_reward = jnp.dot(attended.astype(jnp.float32), reward_weight, precision=lax.Precision.HIGHEST)
        kept = jnp.where(is_end, row_reward, 0.0)
        bin_of = reward_bins[seq_index][segments].astype(jnp.int32)
        local_hist = jnp.zeros((BINS,), jnp.float32).at[bin_of].add(kept)
        return (attended, local_hist)
    attended_all, hist_rows = lax.map(one_sequence, jnp.arange(SEQS, dtype=jnp.int32))
    return (attended_all, lax.optimization_barrier(jnp.sum(hist_rows, axis=0)))
```

```python
import math

import jax
import jax.numpy as jnp
from jax import lax
from jax.experimental import pallas as pl
from jax.experimental.pallas import tpu as pltpu
from jax.sharding import PartitionSpec as P

HQ = 32
HK = 4
HD = 128
GROUP = HQ // HK
BLK = 8
SEGS = 16
BINS = 512
NEG = -1e30
VMEM_BYTES = 40 * 1024 * 1024


def send_slots(dest_ref, count_ref, row, block_count, cap, visit):
    def clear(index, _):
        count_ref[index] = 0
        return 0

    lax.fori_loop(0, dest_ref.shape[0], clear, 0)

    def step(block, _):
        target = dest_ref[row, block]
        rank = count_ref[target]
        count_ref[target] = rank + 1
        visit(block, target * cap + rank)
        return 0

    lax.fori_loop(0, block_count, step, 0)


def sort_kv_kernel(cap, dest_ref, key_ref, value_ref, out_ref, count_ref):
    block_count, _, width = key_ref.shape

    def visit(block, slot):
        for head in range(HK):
            here = slice(head * HD, (head + 1) * HD)
            out_ref[slot, :, 2 * head * HD : (2 * head + 1) * HD] = key_ref[block, :, here]
            out_ref[slot, :, (2 * head + 1) * HD : (2 * head + 2) * HD] = value_ref[block, :, here]

    send_slots(dest_ref, count_ref, lax.axis_index("dp"), block_count, cap, visit)


def sort_query_kernel(cap, dest_ref, query_ref, out_ref, count_ref, sem):
    block_count = query_ref.shape[0]

    def visit(block, slot):
        pltpu.make_async_copy(query_ref.at[block], out_ref.at[slot], sem).start()

    send_slots(dest_ref, count_ref, lax.axis_index("dp"), block_count, cap, visit)
    pltpu.make_async_copy(query_ref, out_ref, sem).wait()


def find_slots(dest_ref, slot_ref, cap):
    dp_count, block_count = dest_ref.shape
    me = lax.axis_index("dp")

    def source(src, _):
        def column(block, rank):
            hit = dest_ref[src, block] == me

            @pl.when(hit)
            def _():
                slot_ref[block] = src * cap + rank

            return rank + jnp.where(hit, 1, 0)

        lax.fori_loop(0, block_count, column, 0)
        return 0

    lax.fori_loop(0, dp_count, source, 0)


def unsort_kv_kernel(cap, dest_ref, seg_ref, got_ref, out_ref, slot_ref):
    find_slots(dest_ref, slot_ref, cap)
    block_count = got_ref.shape[0]
    row_count = block_count * BLK
    for pair in range(block_count // 2):
        rows = jnp.concatenate([got_ref[slot_ref[2 * pair]], got_ref[slot_ref[2 * pair + 1]]], axis=0)
        out_ref[2 * BLK * pair : 2 * BLK * (pair + 1), :] = rows
    labels = seg_ref[...].astype(jnp.float32)
    labels = jnp.concatenate([labels] * (out_ref.shape[1] // row_count), axis=1)
    labels = jnp.broadcast_to(labels, (2 * BLK, out_ref.shape[1]))
    out_ref[row_count:, :] = labels.astype(out_ref.dtype)


def attend_kernel(
    cap,
    part_count,
    dest_ref,
    bins_ref,
    next_ref,
    seg_ref,
    weight_ref,
    query_ref,
    *rest,
):
    part_refs = rest[:part_count]
    out_ref, hist_ref = rest[part_count : part_count + 2]
    slot_ref, bias_ref, key_ref, value_ref, reward_ref = rest[part_count + 2 :]
    step = pl.program_id(0)
    row_count = out_ref.shape[0]
    block_count = row_count // BLK
    ctx_self = lax.axis_index("ctx")
    seg_row = seg_ref[...]
    seg_col = jnp.transpose(jnp.broadcast_to(seg_row, (row_count, row_count)))

    @pl.when(step == 0)
    def _():
        find_slots(dest_ref, slot_ref, cap)
        reward_ref[...] = jnp.zeros_like(reward_ref)
        q_pos = lax.broadcasted_iota(jnp.int32, (row_count, row_count), 0)
        k_pos = lax.broadcasted_iota(jnp.int32, (row_count, row_count), 1)
        own = (seg_col == seg_row) & (k_pos <= q_pos)
        bias_ref[:, :row_count] = jnp.where(own, 0.0, NEG)
        for hop in range(1, part_count):
            labels = part_refs[hop][row_count : row_count + 1, :row_count].astype(jnp.float32)
            there = (seg_col.astype(jnp.float32) == labels) & (ctx_self >= hop)
            bias_ref[:, hop * row_count : (hop + 1) * row_count] = jnp.where(there, 0.0, NEG)

    first = pl.multiple_of(step * 2 * HD, 2 * HD)
    for part in range(part_count):
        rows = slice(part * row_count, (part + 1) * row_count)
        key_ref[rows, :] = part_refs[part][:row_count, pl.ds(first, HD)]
        value_ref[rows, :] = part_refs[part][:row_count, pl.ds(first + HD, HD)]
    keys = key_ref[...]
    values = value_ref[...]
    query = jnp.concatenate([query_ref[slot_ref[block]] for block in range(block_count)], axis=0)
    factor = math.log2(math.e) / math.sqrt(HD)
    reward = reward_ref[...]
    for head in range(GROUP):
        here = slice(head * HD, (head + 1) * HD)
        scores = lax.dot_general(
            query[:, here], keys, (((1,), (1,)), ((), ())), preferred_element_type=jnp.float32
        )
        scores = scores + bias_ref[...]
        top = jnp.max(scores, axis=1, keepdims=True)
        weights = jnp.exp2((scores - top) * factor)
        total = jnp.sum(weights, axis=1, keepdims=True)
        mixed = jnp.dot(weights.astype(jnp.bfloat16), values, preferred_element_type=jnp.float32)
        attended = (mixed / total).astype(jnp.bfloat16)
        out_ref[:, here] = attended
        reward = reward + attended.astype(jnp.float32) * weight_ref[:, here]
    reward_ref[...] = reward

    @pl.when(step == HK - 1)
    def _():
        after = jnp.concatenate([seg_row[:, 1:], jnp.full((1, 1), next_ref[0], jnp.int32)], axis=1)
        after_col = jnp.transpose(jnp.broadcast_to(after, (row_count, row_count)))
        row_reward = jnp.sum(reward_ref[...], axis=1, keepdims=True)
        kept = jnp.where(seg_col != after_col, row_reward, 0.0)
        label = lax.broadcasted_iota(jnp.int32, (row_count, row_count), 1)
        by_seg = jnp.sum(jnp.where(seg_col == label, kept, 0.0), axis=0, keepdims=True)
        bin_id = lax.broadcasted_iota(jnp.int32, (1, BINS), 1)
        hist = jnp.zeros((1, BINS), jnp.float32)
        for seg in range(SEGS):
            hist = hist + jnp.where(bin_id == bins_ref[0, seg], by_seg[:, seg : seg + 1], 0.0)
        hist_ref[...] = jnp.broadcast_to(hist, hist_ref.shape)


def local(roll_query, roll_keys, roll_values, pack_dest, segment_ids, reward_bins, reward_weight):
    dp_count = lax.axis_size("dp")
    ctx_count = lax.axis_size("ctx")
    ctx_self = lax.axis_index("ctx")
    row_count = roll_query.shape[1]
    q_width = roll_query.shape[2]
    kv_width = roll_keys.shape[2]
    block_count = row_count // BLK
    cap = (block_count + dp_count - 1) // dp_count
    slot_count = dp_count * cap
    reach = row_count * ctx_count // 2
    hop_count = min(ctx_count - 1, (reach - 1 + row_count - 1) // row_count)
    smem = pl.BlockSpec(memory_space=pltpu.SMEM)
    vmem = pl.BlockSpec(memory_space=pltpu.VMEM)
    hbm = pl.BlockSpec(memory_space=pl.ANY)
    params = pltpu.CompilerParams(vmem_limit_bytes=VMEM_BYTES)

    sorted_kv = pl.pallas_call(
        lambda *refs: sort_kv_kernel(cap, *refs),
        out_shape=jax.ShapeDtypeStruct((slot_count, BLK, 2 * kv_width), jnp.bfloat16),
        in_specs=[smem, vmem, vmem],
        out_specs=vmem,
        scratch_shapes=[pltpu.SMEM((dp_count,), jnp.int32)],
        compiler_params=params,
        name="sort_kv",
    )(
        pack_dest,
        roll_keys.reshape(block_count, BLK, kv_width),
        roll_values.reshape(block_count, BLK, kv_width),
    )
    got_kv = lax.all_to_all(
        sorted_kv.reshape(dp_count, cap * BLK, 2 * kv_width), "dp", split_axis=0, concat_axis=0, tiled=True
    ).reshape(slot_count, BLK, 2 * kv_width)

    sorted_query = pl.pallas_call(
        lambda *refs: sort_query_kernel(cap, *refs),
        out_shape=jax.ShapeDtypeStruct((slot_count, BLK, q_width), jnp.bfloat16),
        in_specs=[smem, hbm],
        out_specs=hbm,
        scratch_shapes=[pltpu.SMEM((dp_count,), jnp.int32), pltpu.SemaphoreType.DMA],
        compiler_params=params,
        name="sort_query",
    )(pack_dest, roll_query.reshape(block_count, BLK, q_width))
    got_query = lax.all_to_all(
        sorted_query.reshape(dp_count, cap * BLK, q_width), "dp", split_axis=0, concat_axis=0, tiled=True
    ).reshape(slot_count, BLK, q_width)

    parts = [
        pl.pallas_call(
            lambda *refs: unsort_kv_kernel(cap, *refs),
            out_shape=jax.ShapeDtypeStruct((row_count + 2 * BLK, 2 * kv_width), jnp.bfloat16),
            in_specs=[smem, vmem, vmem],
            out_specs=vmem,
            scratch_shapes=[pltpu.SMEM((block_count,), jnp.int32)],
            compiler_params=params,
            name="unsort_kv",
        )(pack_dest, segment_ids, got_kv)
    ]
    forward = [(i, i + 1) for i in range(ctx_count - 1)]
    for _ in range(hop_count):
        parts.append(lax.ppermute(parts[-1], "ctx", forward))
    backward = [(i + 1, i) for i in range(ctx_count - 1)]
    next_first = lax.ppermute(segment_ids[0, :1] + 1, "ctx", backward) - 1

    part_count = len(parts)
    part_spec = pl.BlockSpec((row_count + 2 * BLK, 2 * kv_width), lambda g: (0, 0))
    device_count = dp_count * ctx_count
    attended, hist_rows = pl.pallas_call(
        lambda *refs: attend_kernel(cap, part_count, *refs),
        grid=(HK,),
        out_shape=(
            jax.ShapeDtypeStruct((row_count, q_width), jnp.bfloat16),
            jax.ShapeDtypeStruct((device_count, BINS), jnp.float32),
        ),
        in_specs=[
            smem,
            smem,
            smem,
            pl.BlockSpec((1, row_count), lambda g: (0, 0)),
            pl.BlockSpec((1, GROUP * HD), lambda g: (0, g)),
            pl.BlockSpec((slot_count, BLK, GROUP * HD), lambda g: (0, 0, g)),
        ]
        + [part_spec] * part_count,
        out_specs=(
            pl.BlockSpec((row_count, GROUP * HD), lambda g: (0, g)),
            pl.BlockSpec((device_count, BINS), lambda g: (0, 0)),
        ),
        scratch_shapes=[
            pltpu.SMEM((block_count,), jnp.int32),
            pltpu.VMEM((row_count, part_count * row_count), jnp.float32),
            pltpu.VMEM((part_count * row_count, HD), jnp.bfloat16),
            pltpu.VMEM((part_count * row_count, HD), jnp.bfloat16),
            pltpu.VMEM((row_count, HD), jnp.float32),
        ],
        compiler_params=params,
        name="attend",
    )(pack_dest, reward_bins, next_first, segment_ids, reward_weight.reshape(1, q_width), got_query, *parts)
    gathered = lax.all_to_all(hist_rows, ("dp", "ctx"), split_axis=0, concat_axis=0, tiled=True)
    return attended.reshape(1, row_count, q_width), jnp.sum(gathered, axis=0)


def solution(mesh):
    in_specs = (
        P("dp", "ctx", None),
        P("dp", "ctx", None),
        P("dp", "ctx", None),
        P(None, "ctx"),
        P("dp", "ctx"),
        P("dp", None),
        P(),
    )
    out_specs = (P("dp", "ctx", None), P())
    return jax.shard_map(local, mesh=mesh, in_specs=in_specs, out_specs=out_specs, check_vma=False)
```

```python
import math

import jax
import jax.numpy as jnp
from jax import lax
from jax.experimental import pallas as pl
from jax.experimental.pallas import tpu as pltpu
from jax.sharding import PartitionSpec as P

HQ = 32
HK = 4
HD = 128
GROUP = HQ // HK
BLK = 8
SEGS = 16
BINS = 512
NEG = -1e30
FINISH_HEADS = 2 * GROUP
FACTOR = math.log2(math.e) / math.sqrt(HD)


def params(mebibytes):
    return pltpu.CompilerParams(vmem_limit_bytes=mebibytes * 1024 * 1024)


def cost(flops, nbytes):
    return pl.CostEstimate(flops=flops, bytes_accessed=nbytes, transcendentals=0)


def find_blocks(dest_ref, block_ref, count_ref, cap, relative):
    dp_count, block_count = dest_ref.shape
    me = lax.axis_index("dp")
    for target in range(dp_count):
        count_ref[target] = 0
    for block in range(block_count):
        target = dest_ref[me, block]
        rank = count_ref[target]
        count_ref[target] = rank + 1
        place = (target ^ me) if relative else target
        block_ref[place * cap + rank] = block


def find_columns(dest_ref, column_ref, cap, relative):
    dp_count, block_count = dest_ref.shape
    me = lax.axis_index("dp")

    def source(src, _):
        place = (src ^ me) if relative else src
        rank = 0
        for block in range(block_count):
            hit = dest_ref[src, block] == me

            @pl.when(hit)
            def _():
                column_ref[place * cap + rank] = block

            rank = rank + jnp.where(hit, 1, 0)
        return 0

    lax.fori_loop(0, dp_count, source, 0)


def sort_kv_kernel(cap, dest_hbm, key_hbm, value_hbm, out_ref, *scratch):
    dest_ref, block_ref, count_ref, key_ref, value_ref, stage_ref, in_sem, out_sem = scratch
    arrivals = [
        pltpu.make_async_copy(source, target, in_sem.at[index])
        for index, (source, target) in enumerate(
            ((dest_hbm, dest_ref), (key_hbm, key_ref), (value_hbm, value_ref))
        )
    ]
    for arrival in arrivals:
        arrival.start()
    arrivals[0].wait()
    find_blocks(dest_ref, block_ref, count_ref, cap, False)
    arrivals[1].wait()
    arrivals[2].wait()
    width = key_ref.shape[2]
    for slot in range(out_ref.shape[0]):
        block = block_ref[slot]
        stage_ref[slot, :, :width] = key_ref[block]
        stage_ref[slot, :, width:] = value_ref[block]
    departure = pltpu.make_async_copy(stage_ref, out_ref, out_sem)
    departure.start()
    departure.wait()


def sort_query_kernel(cap, piece_count, dest_ref, query_ref, after_ref, *rest):
    pieces = rest[:piece_count]
    block_ref, count_ref, sem = rest[piece_count:]
    find_blocks(dest_ref, block_ref, count_ref, cap, True)
    copies = []
    for slot in range(2 * piece_count * cap):
        piece, place = divmod(slot, 2 * cap)
        copies.append(
            pltpu.make_async_copy(query_ref.at[block_ref[slot]], pieces[piece].at[place], sem.at[slot])
        )
    for copy in copies:
        copy.start()
    for copy in copies:
        copy.wait()


def merge_kernel(cap, piece_count, *refs):
    pieces, out_ref = refs[:piece_count], refs[piece_count]
    for piece in range(piece_count):
        out_ref[piece * cap : (piece + 1) * cap] = pieces[piece][cap:]


def unsort_query_kernel(cap, piece_count, dest_ref, *rest):
    pieces = rest[:piece_count]
    other_ref, out_ref, column_ref = rest[piece_count:]
    find_columns(dest_ref, column_ref, cap, True)
    for piece in range(piece_count):
        for rank in range(cap):
            out_ref[column_ref[2 * piece * cap + rank]] = pieces[piece][rank]
            out_ref[column_ref[(2 * piece + 1) * cap + rank]] = other_ref[piece * cap + rank]


def unsort_kv_kernel(cap, dest_ref, seg_ref, got_ref, out_ref, column_ref):
    find_columns(dest_ref, column_ref, cap, False)
    block_count = got_ref.shape[0]
    for slot in range(block_count):
        out_ref[column_ref[slot]] = got_ref[slot]
    labels = seg_ref[...].astype(jnp.float32)
    labels = jnp.concatenate([labels] * (out_ref.shape[2] // labels.shape[1]), axis=1)
    out_ref[block_count] = jnp.broadcast_to(labels, out_ref.shape[1:]).astype(out_ref.dtype)


def after_kernel(*refs):
    pass


def rows_of(ref, lane):
    block_count = ref.shape[0] - 1
    return ref[:block_count, :, lane : lane + HD].reshape(block_count * BLK, HD)


def allowed_bias(part_ref, hop, seg_row):
    row_count = seg_row.shape[1]
    square = (row_count, row_count)
    labels = part_ref[part_ref.shape[0] - 1][:1, :row_count].astype(jnp.float32)
    labels = jnp.transpose(jnp.broadcast_to(labels, square))
    allowed = labels == seg_row.astype(jnp.float32)
    if hop == 0:
        key_pos = lax.broadcasted_iota(jnp.int32, square, 0)
        query_pos = lax.broadcasted_iota(jnp.int32, square, 1)
        allowed = allowed & (key_pos <= query_pos)
    else:
        allowed = allowed & (lax.axis_index("ctx") >= hop)
    return jnp.where(allowed, 0.0, NEG)


def score(keys, query_ref, head):
    here = slice(head * HD, (head + 1) * HD)
    query = query_ref[:, :, here].reshape(query_ref.shape[0] * BLK, HD)
    return lax.dot_general(keys, query, (((1,), (1,)), ((), ())), preferred_element_type=jnp.float32)


def begin_kernel(part_count, seg_ref, query_ref, *rest):
    part_refs = rest[:part_count]
    top_ref, total_ref, mixed_ref, bias_ref = rest[part_count:]
    row_count = seg_ref.shape[1]
    for hop in range(part_count):
        bias_ref[hop * row_count : (hop + 1) * row_count, :] = allowed_bias(part_refs[hop], hop, seg_ref[...])
    keys, values = [], []
    for group in range(HK):
        keys.append(jnp.concatenate([rows_of(ref, group * HD) for ref in part_refs], axis=0))
        rows = jnp.concatenate([rows_of(ref, (HK + group) * HD) for ref in part_refs], axis=0)
        values.append(jnp.transpose(rows))
    for first in range(0, HQ, GROUP):
        heads = range(first, first + GROUP)
        scores = [score(keys[head // GROUP], query_ref, head) + bias_ref[...] for head in heads]
        tops = [jnp.max(each, axis=0, keepdims=True) for each in scores]
        weights = [jnp.exp2((each - top) * FACTOR) for each, top in zip(scores, tops)]
        for head, top, each in zip(heads, tops, weights):
            top_ref[head : head + 1, :] = top
            total_ref[head : head + 1, :] = jnp.sum(each, axis=0, keepdims=True)
            mixed_ref[head] = jnp.dot(
                values[head // GROUP], each.astype(jnp.bfloat16), preferred_element_type=jnp.float32
            )


def finish_kernel(hop, bins_ref, seg_ref, weight_ref, query_ref, top_ref, total_ref, mixed_ref, *rest):
    part_ref, out_ref, hist_ref, bias_ref = rest
    row_count = out_ref.shape[0]
    square = (row_count, row_count)
    seg_row = seg_ref[...]
    bias_ref[...] = allowed_bias(part_ref, hop, seg_row)
    reward = jnp.zeros(square, jnp.float32)
    keys = [rows_of(part_ref, group * HD) for group in range(HK)]
    values = [jnp.transpose(rows_of(part_ref, (HK + group) * HD)) for group in range(HK)]
    for first in range(0, HQ, FINISH_HEADS):
        heads = range(first, first + FINISH_HEADS)
        scores = [score(keys[head // GROUP], query_ref, head) + bias_ref[...] for head in heads]
        before = [top_ref[head : head + 1, :] for head in heads]
        tops = [jnp.maximum(old, jnp.max(each, axis=0, keepdims=True)) for old, each in zip(before, scores)]
        weights = [jnp.exp2((each - top) * FACTOR) for each, top in zip(scores, tops)]
        shrinks = [jnp.exp2((old - top) * FACTOR) for old, top in zip(before, tops)]
        totals = [
            total_ref[head : head + 1, :] * shrink + jnp.sum(each, axis=0, keepdims=True)
            for head, shrink, each in zip(heads, shrinks, weights)
        ]
        mixed = [
            jnp.dot(values[head // GROUP], each.astype(jnp.bfloat16), preferred_element_type=jnp.float32)
            for head, each in zip(heads, weights)
        ]
        inverses = [1.0 / total for total in totals]
        mixed = [
            mixed_ref[head] * (shrink * inverse) + each * inverse
            for head, shrink, inverse, each in zip(heads, shrinks, inverses, mixed)
        ]
        attended = [jnp.transpose(each.astype(jnp.bfloat16)) for each in mixed]
        for head, each in zip(heads, attended):
            here = slice(head * HD, (head + 1) * HD)
            out_ref[:, here] = each
            reward = reward + each.astype(jnp.float32) * weight_ref[:, here]

    seg_col = jnp.transpose(jnp.broadcast_to(seg_row, square))
    after = jnp.concatenate([seg_row[:, 1:], seg_row[:, row_count - 1 :]], axis=1)
    after_col = jnp.transpose(jnp.broadcast_to(after, square))
    row_reward = jnp.sum(reward, axis=1, keepdims=True)
    kept = jnp.where(seg_col != after_col, row_reward, 0.0)
    label = lax.broadcasted_iota(jnp.int32, square, 1)
    by_seg = jnp.sum(jnp.where(seg_col == label, kept, 0.0), axis=0, keepdims=True)
    bin_id = lax.broadcasted_iota(jnp.int32, (1, BINS), 1)
    hist = jnp.zeros((1, BINS), jnp.float32)
    last_bin = jnp.zeros((1, 1), jnp.int32)
    last_seg = seg_row[:, row_count - 1 :]
    for seg in range(SEGS):
        hist = hist + jnp.where(bin_id == bins_ref[0, seg], by_seg[:, seg : seg + 1], 0.0)
        last_bin = last_bin + jnp.where(last_seg == seg, bins_ref[0, seg], 0)
    lane = lax.broadcasted_iota(jnp.int32, (1, HD), 1)
    notes = jnp.where(lane == 0, row_reward[row_count - 1 :, :], 0.0)
    notes = notes + jnp.where(lane == 1, last_bin.astype(jnp.float32), 0.0)
    notes = notes + jnp.where(lane == 2, seg_row[:, :1].astype(jnp.float32), 0.0)
    notes = notes + jnp.where(lane == 3, last_seg.astype(jnp.float32), 0.0)
    hist_ref[...] = jnp.broadcast_to(jnp.concatenate([hist, notes], axis=1), hist_ref.shape)


def total_kernel(ctx_count, rows_ref, out_ref):
    device_count = rows_ref.shape[0]
    notes = rows_ref[:, BINS:]
    reward, bin_of, first, last = (notes[:, k : k + 1] for k in range(4))
    following = jnp.concatenate([first[1:], first[:1]], axis=0)
    device = lax.broadcasted_iota(jnp.int32, (device_count, 1), 0)
    ends = (following != last) | (lax.rem(device, ctx_count) == ctx_count - 1)
    bin_id = lax.broadcasted_iota(jnp.int32, (device_count, BINS), 1).astype(jnp.float32)
    extra = jnp.where((bin_id == bin_of) & ends, reward, 0.0)
    out_ref[...] = jnp.sum(rows_ref[:, :BINS] + extra, axis=0, keepdims=True)


def local(roll_query, roll_keys, roll_values, pack_dest, segment_ids, reward_bins, reward_weight):
    dp_count = lax.axis_size("dp")
    ctx_count = lax.axis_size("ctx")
    row_count = roll_query.shape[1]
    q_width = roll_query.shape[2]
    kv_width = roll_keys.shape[2]
    block_count = row_count // BLK
    cap = (block_count + dp_count - 1) // dp_count
    slot_count = dp_count * cap
    piece_count = dp_count // 2
    reach = row_count * ctx_count // 2
    hop_count = min(ctx_count - 1, (reach - 1 + row_count - 1) // row_count)
    device_count = dp_count * ctx_count
    smem = pl.BlockSpec(memory_space=pltpu.SMEM)
    vmem = pl.BlockSpec(memory_space=pltpu.VMEM)
    hbm = pl.BlockSpec(memory_space=pl.ANY)

    def across(array, distance):
        return lax.ppermute(array, "dp", [(i, i ^ distance) for i in range(dp_count)])

    def gather(pieces, width, name, **options):
        pieces = [pieces[0]] + [across(pieces[i], 2 * i) for i in range(1, piece_count)]
        other = pl.pallas_call(
            lambda *refs: merge_kernel(cap, piece_count, *refs),
            out_shape=jax.ShapeDtypeStruct((piece_count * cap, BLK, width), jnp.bfloat16),
            in_specs=[vmem] * piece_count,
            out_specs=vmem,
            compiler_params=params(16),
            name=name,
        )(*pieces)
        return pieces + [across(other, 1)]

    sorted_kv = pl.pallas_call(
        lambda *refs: sort_kv_kernel(cap, *refs),
        out_shape=jax.ShapeDtypeStruct((slot_count, BLK, 2 * kv_width), jnp.bfloat16),
        in_specs=[hbm, hbm, hbm],
        out_specs=hbm,
        scratch_shapes=[
            pltpu.SMEM((dp_count, block_count), jnp.int32),
            pltpu.SMEM((slot_count,), jnp.int32),
            pltpu.SMEM((dp_count,), jnp.int32),
            pltpu.VMEM((block_count, BLK, kv_width), jnp.bfloat16),
            pltpu.VMEM((block_count, BLK, kv_width), jnp.bfloat16),
            pltpu.VMEM((slot_count, BLK, 2 * kv_width), jnp.bfloat16),
            pltpu.SemaphoreType.DMA((3,)),
            pltpu.SemaphoreType.DMA,
        ],
        compiler_params=params(60),
        name="sort_kv",
    )(
        pack_dest,
        roll_keys.reshape(block_count, BLK, kv_width),
        roll_values.reshape(block_count, BLK, kv_width),
    )
    got_kv = lax.all_to_all(
        sorted_kv.reshape(dp_count, cap * BLK, 2 * kv_width), "dp", split_axis=0, concat_axis=0, tiled=True
    ).reshape(slot_count, BLK, 2 * kv_width)

    sorted_query = pl.pallas_call(
        lambda *refs: sort_query_kernel(cap, piece_count, *refs),
        out_shape=[jax.ShapeDtypeStruct((2 * cap, BLK, q_width), jnp.bfloat16)] * piece_count,
        in_specs=[smem, hbm, hbm],
        out_specs=[hbm] * piece_count,
        scratch_shapes=[
            pltpu.SMEM((slot_count,), jnp.int32),
            pltpu.SMEM((dp_count,), jnp.int32),
            pltpu.SemaphoreType.DMA((slot_count,)),
        ],
        compiler_params=params(16),
        name="sort_query",
    )(pack_dest, roll_query.reshape(block_count, BLK, q_width), sorted_kv)
    sorted_query = pl.pallas_call(
        after_kernel,
        out_shape=[jax.ShapeDtypeStruct((2 * cap, BLK, q_width), jnp.bfloat16)] * piece_count,
        in_specs=[hbm] * (piece_count + 1),
        out_specs=[hbm] * piece_count,
        input_output_aliases={i: i for i in range(piece_count)},
        compiler_params=params(1),
        name="after_kv",
    )(*sorted_query, got_kv)
    got_query = gather(sorted_query, q_width, "merge_query")
    query = pl.pallas_call(
        lambda *refs: unsort_query_kernel(cap, piece_count, *refs),
        out_shape=jax.ShapeDtypeStruct((block_count, BLK, q_width), jnp.bfloat16),
        in_specs=[smem] + [vmem] * (piece_count + 1),
        out_specs=vmem,
        scratch_shapes=[pltpu.SMEM((slot_count,), jnp.int32)],
        compiler_params=params(16),
        name="unsort_query",
    )(pack_dest, *got_query)

    own = pl.pallas_call(
        lambda *refs: unsort_kv_kernel(cap, *refs),
        out_shape=jax.ShapeDtypeStruct((block_count + 1, BLK, 2 * kv_width), jnp.bfloat16),
        in_specs=[smem, vmem, vmem],
        out_specs=vmem,
        scratch_shapes=[pltpu.SMEM((slot_count,), jnp.int32)],
        compiler_params=params(16),
        name="unsort_kv",
    )(pack_dest, segment_ids, got_kv)
    parts = [own]
    forward = [(i, i + 1) for i in range(ctx_count - 1)]
    for _ in range(hop_count):
        parts.append(lax.ppermute(parts[-1], "ctx", forward))

    state = pl.pallas_call(
        lambda *refs: begin_kernel(hop_count, *refs),
        out_shape=(
            jax.ShapeDtypeStruct((HQ, row_count), jnp.float32),
            jax.ShapeDtypeStruct((HQ, row_count), jnp.float32),
            jax.ShapeDtypeStruct((HQ, HD, row_count), jnp.float32),
        ),
        in_specs=[vmem] * (2 + hop_count),
        out_specs=(vmem, vmem, vmem),
        scratch_shapes=[pltpu.VMEM((hop_count * row_count, row_count), jnp.float32)],
        compiler_params=params(16),
        name="begin",
    )(segment_ids, query, *parts[:-1])
    attended, hist_rows = pl.pallas_call(
        lambda *refs: finish_kernel(hop_count, *refs),
        out_shape=(
            jax.ShapeDtypeStruct((row_count, q_width), jnp.bfloat16),
            jax.ShapeDtypeStruct((device_count, BINS + HD), jnp.float32),
        ),
        in_specs=[smem] + [vmem] * 7,
        out_specs=(vmem, vmem),
        scratch_shapes=[pltpu.VMEM((row_count, row_count), jnp.float32)],
        compiler_params=params(16),
        name="finish",
    )(reward_bins, segment_ids, reward_weight.reshape(1, q_width), query, *state, parts[-1])
    gathered = lax.all_to_all(hist_rows, ("dp", "ctx"), split_axis=0, concat_axis=0, tiled=True)
    total = pl.pallas_call(
        lambda *refs: total_kernel(ctx_count, *refs),
        out_shape=jax.ShapeDtypeStruct((1, BINS), jnp.float32),
        in_specs=[vmem],
        out_specs=vmem,
        compiler_params=params(16),
        name="total",
    )(gathered)
    return attended.reshape(1, row_count, q_width), total.reshape(BINS)


def solution(mesh):
    in_specs = (
        P("dp", "ctx", None),
        P("dp", "ctx", None),
        P("dp", "ctx", None),
        P(None, "ctx"),
        P("dp", "ctx"),
        P("dp", None),
        P(),
    )
    out_specs = (P("dp", "ctx", None), P())
    return jax.shard_map(local, mesh=mesh, in_specs=in_specs, out_specs=out_specs, check_vma=False)
```

```python
import math

import jax
import jax.numpy as jnp
from jax import lax
from jax.experimental import pallas as pl
from jax.experimental.pallas import tpu as pltpu
from jax.sharding import PartitionSpec as P

HQ = 32
HK = 4
HD = 128
GROUP = HQ // HK
BLK = 8
SEGS = 16
BINS = 512
NEG = -1e30
FINISH_HEADS = 2 * GROUP
FACTOR = math.log2(math.e) / math.sqrt(HD)


def params(mebibytes):
    return pltpu.CompilerParams(vmem_limit_bytes=mebibytes * 1024 * 1024)


def cost(flops, nbytes):
    return pl.CostEstimate(flops=flops, bytes_accessed=nbytes, transcendentals=0)


def find_blocks(dest_ref, block_ref, count_ref, cap, relative):
    dp_count, block_count = dest_ref.shape
    me = lax.axis_index("dp")
    for target in range(dp_count):
        count_ref[target] = 0
    for block in range(block_count):
        target = dest_ref[me, block]
        rank = count_ref[target]
        count_ref[target] = rank + 1
        place = (target ^ me) if relative else target
        block_ref[place * cap + rank] = block


def find_columns(dest_ref, column_ref, cap, relative):
    dp_count, block_count = dest_ref.shape
    me = lax.axis_index("dp")

    def source(src, _):
        place = (src ^ me) if relative else src
        rank = 0
        for block in range(block_count):
            hit = dest_ref[src, block] == me

            @pl.when(hit)
            def _():
                column_ref[place * cap + rank] = block

            rank = rank + jnp.where(hit, 1, 0)
        return 0

    lax.fori_loop(0, dp_count, source, 0)


def sort_kv_kernel(cap, dest_hbm, key_hbm, value_hbm, out_ref, *scratch):
    dest_ref, block_ref, count_ref, key_ref, value_ref, stage_ref, in_sem, out_sem = scratch
    arrivals = [
        pltpu.make_async_copy(source, target, in_sem.at[index])
        for index, (source, target) in enumerate(
            ((dest_hbm, dest_ref), (key_hbm, key_ref), (value_hbm, value_ref))
        )
    ]
    for arrival in arrivals:
        arrival.start()
    arrivals[0].wait()
    find_blocks(dest_ref, block_ref, count_ref, cap, False)
    arrivals[1].wait()
    arrivals[2].wait()
    width = key_ref.shape[2]
    for slot in range(out_ref.shape[0]):
        block = block_ref[slot]
        stage_ref[slot, :, :width] = key_ref[block]
        stage_ref[slot, :, width:] = value_ref[block]
    departure = pltpu.make_async_copy(stage_ref, out_ref, out_sem)
    departure.start()
    departure.wait()


def sort_query_kernel(cap, piece_count, dest_hbm, query_hbm, *rest):
    pieces = rest[:piece_count]
    dest_ref, block_ref, count_ref, query_ref, in_sem, out_sem = rest[piece_count:]
    arrivals = [
        pltpu.make_async_copy(dest_hbm, dest_ref, in_sem.at[0]),
        pltpu.make_async_copy(query_hbm, query_ref, in_sem.at[1]),
    ]
    for arrival in arrivals:
        arrival.start()
    arrivals[0].wait()
    find_blocks(dest_ref, block_ref, count_ref, cap, True)
    arrivals[1].wait()
    departures = []
    for slot in range(2 * piece_count * cap):
        piece, place = divmod(slot, 2 * cap)
        departures.append(
            pltpu.make_async_copy(query_ref.at[block_ref[slot]], pieces[piece].at[place], out_sem.at[slot])
        )
    for departure in departures:
        departure.start()
    for departure in departures:
        departure.wait()


def merge_kernel(cap, piece_count, *refs):
    pieces, out_ref = refs[:piece_count], refs[piece_count]
    for piece in range(piece_count):
        out_ref[piece * cap : (piece + 1) * cap] = pieces[piece][cap:]


def unsort_query_kernel(cap, piece_count, dest_ref, *rest):
    pieces = rest[:piece_count]
    other_ref, out_ref, column_ref = rest[piece_count:]
    find_columns(dest_ref, column_ref, cap, True)
    for piece in range(piece_count):
        for rank in range(cap):
            out_ref[column_ref[2 * piece * cap + rank]] = pieces[piece][rank]
            out_ref[column_ref[(2 * piece + 1) * cap + rank]] = other_ref[piece * cap + rank]


def unsort_kv_kernel(cap, dest_ref, seg_ref, got_ref, out_ref, column_ref):
    find_columns(dest_ref, column_ref, cap, False)
    block_count = got_ref.shape[0]
    for slot in range(block_count):
        out_ref[column_ref[slot]] = got_ref[slot]
    labels = seg_ref[...].astype(jnp.float32)
    labels = jnp.concatenate([labels] * (out_ref.shape[2] // labels.shape[1]), axis=1)
    out_ref[block_count] = jnp.broadcast_to(labels, out_ref.shape[1:]).astype(out_ref.dtype)


def rows_of(ref, lane):
    block_count = ref.shape[0] - 1
    return ref[:block_count, :, lane : lane + HD].reshape(block_count * BLK, HD)


def allowed_bias(part_ref, hop, seg_row):
    row_count = seg_row.shape[1]
    square = (row_count, row_count)
    labels = part_ref[part_ref.shape[0] - 1][:1, :row_count].astype(jnp.float32)
    labels = jnp.transpose(jnp.broadcast_to(labels, square))
    allowed = labels == seg_row.astype(jnp.float32)
    if hop == 0:
        key_pos = lax.broadcasted_iota(jnp.int32, square, 0)
        query_pos = lax.broadcasted_iota(jnp.int32, square, 1)
        allowed = allowed & (key_pos <= query_pos)
    else:
        allowed = allowed & (lax.axis_index("ctx") >= hop)
    return jnp.where(allowed, 0.0, NEG)


def score(keys, query_ref, head):
    here = slice(head * HD, (head + 1) * HD)
    query = query_ref[:, :, here].reshape(query_ref.shape[0] * BLK, HD)
    return lax.dot_general(keys, query, (((1,), (1,)), ((), ())), preferred_element_type=jnp.float32)


def begin_kernel(part_count, seg_ref, query_ref, *rest):
    part_refs = rest[:part_count]
    top_ref, total_ref, mixed_ref, bias_ref = rest[part_count:]
    row_count = seg_ref.shape[1]
    for hop in range(part_count):
        bias_ref[hop * row_count : (hop + 1) * row_count, :] = allowed_bias(part_refs[hop], hop, seg_ref[...])
    keys, values = [], []
    for group in range(HK):
        keys.append(jnp.concatenate([rows_of(ref, group * HD) for ref in part_refs], axis=0))
        rows = jnp.concatenate([rows_of(ref, (HK + group) * HD) for ref in part_refs], axis=0)
        values.append(jnp.transpose(rows))
    for first in range(0, HQ, GROUP):
        heads = range(first, first + GROUP)
        scores = [score(keys[head // GROUP], query_ref, head) + bias_ref[...] for head in heads]
        tops = [jnp.max(each, axis=0, keepdims=True) for each in scores]
        weights = [jnp.exp2((each - top) * FACTOR) for each, top in zip(scores, tops)]
        for head, top, each in zip(heads, tops, weights):
            top_ref[head : head + 1, :] = top
            total_ref[head : head + 1, :] = jnp.sum(each, axis=0, keepdims=True)
            mixed_ref[head] = jnp.dot(
                values[head // GROUP], each.astype(jnp.bfloat16), preferred_element_type=jnp.float32
            )


def finish_kernel(hop, bins_ref, seg_ref, weight_ref, query_ref, top_ref, total_ref, mixed_ref, *rest):
    part_ref, out_ref, hist_ref, bias_ref = rest
    row_count = out_ref.shape[0]
    square = (row_count, row_count)
    seg_row = seg_ref[...]
    bias_ref[...] = allowed_bias(part_ref, hop, seg_row)
    reward = jnp.zeros(square, jnp.float32)
    keys = [rows_of(part_ref, group * HD) for group in range(HK)]
    values = [jnp.transpose(rows_of(part_ref, (HK + group) * HD)) for group in range(HK)]
    for first in range(0, HQ, FINISH_HEADS):
        heads = range(first, first + FINISH_HEADS)
        scores = [score(keys[head // GROUP], query_ref, head) + bias_ref[...] for head in heads]
        before = [top_ref[head : head + 1, :] for head in heads]
        tops = [jnp.maximum(old, jnp.max(each, axis=0, keepdims=True)) for old, each in zip(before, scores)]
        weights = [jnp.exp2((each - top) * FACTOR) for each, top in zip(scores, tops)]
        shrinks = [jnp.exp2((old - top) * FACTOR) for old, top in zip(before, tops)]
        totals = [
            total_ref[head : head + 1, :] * shrink + jnp.sum(each, axis=0, keepdims=True)
            for head, shrink, each in zip(heads, shrinks, weights)
        ]
        mixed = [
            jnp.dot(values[head // GROUP], each.astype(jnp.bfloat16), preferred_element_type=jnp.float32)
            for head, each in zip(heads, weights)
        ]
        inverses = [1.0 / total for total in totals]
        mixed = [
            mixed_ref[head] * (shrink * inverse) + each * inverse
            for head, shrink, inverse, each in zip(heads, shrinks, inverses, mixed)
        ]
        attended = [jnp.transpose(each.astype(jnp.bfloat16)) for each in mixed]
        for head, each in zip(heads, attended):
            here = slice(head * HD, (head + 1) * HD)
            out_ref[:, here] = each
            reward = reward + each.astype(jnp.float32) * weight_ref[:, here]

    seg_col = jnp.transpose(jnp.broadcast_to(seg_row, square))
    after = jnp.concatenate([seg_row[:, 1:], seg_row[:, row_count - 1 :]], axis=1)
    after_col = jnp.transpose(jnp.broadcast_to(after, square))
    row_reward = jnp.sum(reward, axis=1, keepdims=True)
    kept = jnp.where(seg_col != after_col, row_reward, 0.0)
    label = lax.broadcasted_iota(jnp.int32, square, 1)
    by_seg = jnp.sum(jnp.where(seg_col == label, kept, 0.0), axis=0, keepdims=True)
    bin_id = lax.broadcasted_iota(jnp.int32, (1, BINS), 1)
    hist = jnp.zeros((1, BINS), jnp.float32)
    last_bin = jnp.zeros((1, 1), jnp.int32)
    last_seg = seg_row[:, row_count - 1 :]
    for seg in range(SEGS):
        hist = hist + jnp.where(bin_id == bins_ref[0, seg], by_seg[:, seg : seg + 1], 0.0)
        last_bin = last_bin + jnp.where(last_seg == seg, bins_ref[0, seg], 0)
    lane = lax.broadcasted_iota(jnp.int32, (1, HD), 1)
    notes = jnp.where(lane == 0, row_reward[row_count - 1 :, :], 0.0)
    notes = notes + jnp.where(lane == 1, last_bin.astype(jnp.float32), 0.0)
    notes = notes + jnp.where(lane == 2, seg_row[:, :1].astype(jnp.float32), 0.0)
    notes = notes + jnp.where(lane == 3, last_seg.astype(jnp.float32), 0.0)
    hist_ref[...] = jnp.broadcast_to(jnp.concatenate([hist, notes], axis=1), hist_ref.shape)


def total_kernel(ctx_count, rows_ref, out_ref):
    device_count = rows_ref.shape[0]
    notes = rows_ref[:, BINS:]
    reward, bin_of, first, last = (notes[:, k : k + 1] for k in range(4))
    following = jnp.concatenate([first[1:], first[:1]], axis=0)
    device = lax.broadcasted_iota(jnp.int32, (device_count, 1), 0)
    ends = (following != last) | (lax.rem(device, ctx_count) == ctx_count - 1)
    bin_id = lax.broadcasted_iota(jnp.int32, (device_count, BINS), 1).astype(jnp.float32)
    extra = jnp.where((bin_id == bin_of) & ends, reward, 0.0)
    out_ref[...] = jnp.sum(rows_ref[:, :BINS] + extra, axis=0, keepdims=True)


def local(roll_query, roll_keys, roll_values, pack_dest, segment_ids, reward_bins, reward_weight):
    dp_count = lax.axis_size("dp")
    ctx_count = lax.axis_size("ctx")
    row_count = roll_query.shape[1]
    q_width = roll_query.shape[2]
    kv_width = roll_keys.shape[2]
    block_count = row_count // BLK
    cap = (block_count + dp_count - 1) // dp_count
    slot_count = dp_count * cap
    piece_count = dp_count // 2
    reach = row_count * ctx_count // 2
    hop_count = min(ctx_count - 1, (reach - 1 + row_count - 1) // row_count)
    device_count = dp_count * ctx_count
    smem = pl.BlockSpec(memory_space=pltpu.SMEM)
    vmem = pl.BlockSpec(memory_space=pltpu.VMEM)
    hbm = pl.BlockSpec(memory_space=pl.ANY)

    def across(array, distance):
        return lax.ppermute(array, "dp", [(i, i ^ distance) for i in range(dp_count)])

    def gather(pieces, width, name, **options):
        pieces = [pieces[0]] + [across(pieces[i], 2 * i) for i in range(1, piece_count)]
        other = pl.pallas_call(
            lambda *refs: merge_kernel(cap, piece_count, *refs),
            out_shape=jax.ShapeDtypeStruct((piece_count * cap, BLK, width), jnp.bfloat16),
            in_specs=[vmem] * piece_count,
            out_specs=vmem,
            compiler_params=params(16),
            name=name,
        )(*pieces)
        return pieces + [across(other, 1)]

    sorted_kv = pl.pallas_call(
        lambda *refs: sort_kv_kernel(cap, *refs),
        out_shape=jax.ShapeDtypeStruct((slot_count, BLK, 2 * kv_width), jnp.bfloat16),
        in_specs=[hbm, hbm, hbm],
        out_specs=hbm,
        scratch_shapes=[
            pltpu.SMEM((dp_count, block_count), jnp.int32),
            pltpu.SMEM((slot_count,), jnp.int32),
            pltpu.SMEM((dp_count,), jnp.int32),
            pltpu.VMEM((block_count, BLK, kv_width), jnp.bfloat16),
            pltpu.VMEM((block_count, BLK, kv_width), jnp.bfloat16),
            pltpu.VMEM((slot_count, BLK, 2 * kv_width), jnp.bfloat16),
            pltpu.SemaphoreType.DMA((3,)),
            pltpu.SemaphoreType.DMA,
        ],
        compiler_params=params(60),
        name="sort_kv",
    )(
        pack_dest,
        roll_keys.reshape(block_count, BLK, kv_width),
        roll_values.reshape(block_count, BLK, kv_width),
    )
    got_kv = lax.all_to_all(
        sorted_kv.reshape(dp_count, cap * BLK, 2 * kv_width), "dp", split_axis=0, concat_axis=0, tiled=True
    ).reshape(slot_count, BLK, 2 * kv_width)

    sorted_query = pl.pallas_call(
        lambda *refs: sort_query_kernel(cap, piece_count, *refs),
        out_shape=[jax.ShapeDtypeStruct((2 * cap, BLK, q_width), jnp.bfloat16)] * piece_count,
        in_specs=[hbm, hbm],
        out_specs=[hbm] * piece_count,
        scratch_shapes=[
            pltpu.SMEM((dp_count, block_count), jnp.int32),
            pltpu.SMEM((slot_count,), jnp.int32),
            pltpu.SMEM((dp_count,), jnp.int32),
            pltpu.VMEM((block_count, BLK, q_width), jnp.bfloat16),
            pltpu.SemaphoreType.DMA((2,)),
            pltpu.SemaphoreType.DMA((slot_count,)),
        ],
        compiler_params=params(60),
        name="sort_query",
    )(pack_dest, roll_query.reshape(block_count, BLK, q_width))
    got_query = gather(sorted_query, q_width, "merge_query")
    query = pl.pallas_call(
        lambda *refs: unsort_query_kernel(cap, piece_count, *refs),
        out_shape=jax.ShapeDtypeStruct((block_count, BLK, q_width), jnp.bfloat16),
        in_specs=[smem] + [vmem] * (piece_count + 1),
        out_specs=vmem,
        scratch_shapes=[pltpu.SMEM((slot_count,), jnp.int32)],
        compiler_params=params(16),
        name="unsort_query",
    )(pack_dest, *got_query)

    own = pl.pallas_call(
        lambda *refs: unsort_kv_kernel(cap, *refs),
        out_shape=jax.ShapeDtypeStruct((block_count + 1, BLK, 2 * kv_width), jnp.bfloat16),
        in_specs=[smem, vmem, vmem],
        out_specs=vmem,
        scratch_shapes=[pltpu.SMEM((slot_count,), jnp.int32)],
        compiler_params=params(16),
        cost_estimate=cost(23000000000, 0),
        name="unsort_kv",
    )(pack_dest, segment_ids, got_kv)
    parts = [own]
    forward = [(i, i + 1) for i in range(ctx_count - 1)]
    for _ in range(hop_count):
        parts.append(lax.ppermute(parts[-1], "ctx", forward))

    state = pl.pallas_call(
        lambda *refs: begin_kernel(hop_count, *refs),
        out_shape=(
            jax.ShapeDtypeStruct((HQ, row_count), jnp.float32),
            jax.ShapeDtypeStruct((HQ, row_count), jnp.float32),
            jax.ShapeDtypeStruct((HQ, HD, row_count), jnp.float32),
        ),
        in_specs=[vmem] * (2 + hop_count),
        out_specs=(vmem, vmem, vmem),
        scratch_shapes=[pltpu.VMEM((hop_count * row_count, row_count), jnp.float32)],
        compiler_params=params(16),
        name="begin",
    )(segment_ids, query, *parts[:-1])
    attended, hist_rows = pl.pallas_call(
        lambda *refs: finish_kernel(hop_count, *refs),
        out_shape=(
            jax.ShapeDtypeStruct((row_count, q_width), jnp.bfloat16),
            jax.ShapeDtypeStruct((device_count, BINS + HD), jnp.float32),
        ),
        in_specs=[smem] + [vmem] * 7,
        out_specs=(vmem, vmem),
        scratch_shapes=[pltpu.VMEM((row_count, row_count), jnp.float32)],
        compiler_params=params(16),
        name="finish",
    )(reward_bins, segment_ids, reward_weight.reshape(1, q_width), query, *state, parts[-1])
    gathered = lax.all_to_all(hist_rows, ("dp", "ctx"), split_axis=0, concat_axis=0, tiled=True)
    total = pl.pallas_call(
        lambda *refs: total_kernel(ctx_count, *refs),
        out_shape=jax.ShapeDtypeStruct((1, BINS), jnp.float32),
        in_specs=[vmem],
        out_specs=vmem,
        compiler_params=params(16),
        name="total",
    )(gathered)
    return attended.reshape(1, row_count, q_width), total.reshape(BINS)


def solution(mesh):
    in_specs = (
        P("dp", "ctx", None),
        P("dp", "ctx", None),
        P("dp", "ctx", None),
        P(None, "ctx"),
        P("dp", "ctx"),
        P("dp", None),
        P(),
    )
    out_specs = (P("dp", "ctx", None), P())
    return jax.shard_map(local, mesh=mesh, in_specs=in_specs, out_specs=out_specs, check_vma=False)
```

```python
import math

import jax
import jax.numpy as jnp
from jax import lax
from jax.experimental import pallas as pl
from jax.experimental.pallas import tpu as pltpu
from jax.sharding import PartitionSpec as P

HQ = 32
HK = 4
HD = 128
GROUP = HQ // HK
BLK = 8
SEGS = 16
BINS = 512
NEG = -1e30
SHARES = (2, HK - 2)
FACTOR = math.log2(math.e) / math.sqrt(HD)


def params(mebibytes):
    return pltpu.CompilerParams(vmem_limit_bytes=mebibytes * 1024 * 1024)


def cost(flops, nbytes):
    return pl.CostEstimate(flops=flops, bytes_accessed=nbytes, transcendentals=0)


def find_blocks(dest_ref, block_ref, count_ref, cap, relative):
    dp_count, block_count = dest_ref.shape
    me = lax.axis_index("dp")
    for target in range(dp_count):
        count_ref[target] = 0
    for block in range(block_count):
        target = dest_ref[me, block]
        rank = count_ref[target]
        count_ref[target] = rank + 1
        place = (target ^ me) if relative else target
        block_ref[place * cap + rank] = block


def find_columns(dest_ref, column_ref, cap, relative):
    dp_count, block_count = dest_ref.shape
    me = lax.axis_index("dp")

    def source(src, _):
        place = (src ^ me) if relative else src
        rank = 0
        for block in range(block_count):
            hit = dest_ref[src, block] == me

            @pl.when(hit)
            def _():
                column_ref[place * cap + rank] = block

            rank = rank + jnp.where(hit, 1, 0)
        return 0

    lax.fori_loop(0, dp_count, source, 0)


def sort_kernel(cap, piece_count, dest_hbm, key_hbm, value_hbm, query_hbm, kv_hbm, same_hbm, other_hbm, *scratch):
    dest_ref, block_ref, count_ref, place_ref, key_ref, value_ref, query_ref, stage_ref, in_sem, out_sem = scratch
    arrivals = [
        pltpu.make_async_copy(source, target, in_sem.at[index])
        for index, (source, target) in enumerate(
            ((dest_hbm, dest_ref), (key_hbm, key_ref), (value_hbm, value_ref), (query_hbm, query_ref))
        )
    ]
    for arrival in arrivals:
        arrival.start()
    arrivals[0].wait()
    find_blocks(dest_ref, block_ref, count_ref, cap, False)
    find_blocks(dest_ref, place_ref, count_ref, cap, True)
    arrivals[1].wait()
    arrivals[2].wait()
    width = key_ref.shape[2]
    slot_count = kv_hbm.shape[0]
    for slot in range(slot_count):
        block = block_ref[slot]
        stage_ref[slot, :, :width] = key_ref[block]
        stage_ref[slot, :, width:] = value_ref[block]
    departures = [pltpu.make_async_copy(stage_ref, kv_hbm, out_sem.at[slot_count])]
    departures[0].start()
    arrivals[3].wait()
    for odd, out in ((1, other_hbm), (0, same_hbm)):
        for place in range(piece_count * cap):
            slot = (2 * (place // cap) + odd) * cap + place % cap
            departure = pltpu.make_async_copy(query_ref.at[place_ref[slot]], out.at[place], out_sem.at[slot])
            departure.start()
            departures.append(departure)
    for departure in departures:
        departure.wait()


def merge_query_kernel(cap, piece_count, same_ref, other_ref, *pieces):
    for piece in range(piece_count):
        rows = slice(piece * cap, (piece + 1) * cap)
        pieces[piece][:cap] = same_ref[rows]
        pieces[piece][cap:] = other_ref[rows]


def unsort_query_kernel(cap, piece_count, dest_ref, *rest):
    pieces = rest[:piece_count]
    out_ref, column_ref = rest[piece_count:]
    find_columns(dest_ref, column_ref, cap, True)
    for piece in range(piece_count):
        for place in range(2 * cap):
            out_ref[column_ref[2 * piece * cap + place]] = pieces[piece][place]


def unsort_kv_kernel(cap, dest_ref, seg_ref, got_ref, *rest):
    outs, column_ref = rest[:-1], rest[-1]
    find_columns(dest_ref, column_ref, cap, False)
    block_count = got_ref.shape[0]
    for slot in range(block_count):
        column = column_ref[slot]
        first = 0
        for out_ref, groups in zip(outs, SHARES):
            width = groups * HD
            for half in range(2):
                start = half * HK * HD + first
                out_ref[column, :, half * width : (half + 1) * width] = got_ref[slot, :, start : start + width]
            first += width
    labels = seg_ref[...].astype(jnp.float32)
    labels = jnp.concatenate([labels] * (outs[0].shape[2] // labels.shape[1]), axis=1)
    outs[0][block_count] = jnp.broadcast_to(labels, outs[0].shape[1:]).astype(outs[0].dtype)


def after_kernel(*refs):
    pass


def rows_of(ref, block_count, lane):
    return ref[:block_count, :, lane : lane + HD].reshape(block_count * BLK, HD)


def allowed_bias(label_ref, hop, seg_row):
    row_count = seg_row.shape[1]
    square = (row_count, row_count)
    labels = label_ref[label_ref.shape[0] - 1][:1, :row_count].astype(jnp.float32)
    labels = jnp.transpose(jnp.broadcast_to(labels, square))
    allowed = labels == seg_row.astype(jnp.float32)
    if hop == 0:
        key_pos = lax.broadcasted_iota(jnp.int32, square, 0)
        query_pos = lax.broadcasted_iota(jnp.int32, square, 1)
        allowed = allowed & (key_pos <= query_pos)
    else:
        allowed = allowed & (lax.axis_index("ctx") >= hop)
    return jnp.where(allowed, 0.0, NEG)


def score(keys, query_ref, head):
    here = slice(head * HD, (head + 1) * HD)
    query = query_ref[:, :, here].reshape(query_ref.shape[0] * BLK, HD)
    return lax.dot_general(keys, query, (((1,), (1,)), ((), ())), preferred_element_type=jnp.float32)


def attend_share(share, weight_ref, query_ref, parts, out_ref, bias_ref):
    block_count = query_ref.shape[0]
    before = sum(SHARES[:share])
    reward = jnp.zeros((block_count * BLK, HD), jnp.float32)
    for index in range(SHARES[share]):
        lane = index * HD
        keys = jnp.concatenate([rows_of(part, block_count, lane) for part in parts], axis=0)
        lane = (SHARES[share] + index) * HD
        values = jnp.concatenate([rows_of(part, block_count, lane) for part in parts], axis=0)
        values = jnp.transpose(values)
        heads = range((before + index) * GROUP, (before + index + 1) * GROUP)
        scores = [score(keys, query_ref, head) + bias_ref[...] for head in heads]
        tops = [jnp.max(each, axis=0, keepdims=True) for each in scores]
        weights = [jnp.exp2((each - top) * FACTOR) for each, top in zip(scores, tops)]
        totals = [jnp.sum(each, axis=0, keepdims=True) for each in weights]
        mixed = [
            jnp.dot(values, each.astype(jnp.bfloat16), preferred_element_type=jnp.float32) for each in weights
        ]
        mixed = [each * (1.0 / total) for each, total in zip(mixed, totals)]
        attended = [jnp.transpose(each.astype(jnp.bfloat16)) for each in mixed]
        for head, each in zip(heads, attended):
            first = (head - before * GROUP) * HD
            out_ref[:, first : first + HD] = each
            reward = reward + each.astype(jnp.float32) * weight_ref[:, head * HD : (head + 1) * HD]
    return reward


def first_kernel(bins_ref, seg_ref, weight_ref, query_ref, *rest):
    parts, (out_ref, reward_ref, bias_ref, bin_ref) = rest[:-4], rest[-4:]
    row_count = seg_ref.shape[1]
    for hop, part in enumerate(parts):
        bias_ref[hop * row_count : (hop + 1) * row_count, :] = allowed_bias(part, hop, seg_ref[...])
    reward_ref[...] = attend_share(0, weight_ref, query_ref, parts, out_ref, bias_ref)
    lane = lax.broadcasted_iota(jnp.int32, (1, bin_ref.shape[1]), 1)
    for seg in range(SEGS):
        bin_ref[seg : seg + 1, :] = jnp.where(lane == bins_ref[0, seg], 1.0, 0.0)


def last_kernel(seg_ref, weight_ref, query_ref, before_ref, reward_ref, bias_ref, bin_ref, *rest):
    parts, (out_ref, hist_ref) = rest[:-2], rest[-2:]
    row_count = seg_ref.shape[1]
    square = (row_count, row_count)
    seg_row = seg_ref[...]
    reward = reward_ref[...] + attend_share(1, weight_ref, query_ref, parts, out_ref, bias_ref)

    seg_col = jnp.transpose(jnp.broadcast_to(seg_row, square))
    after = jnp.concatenate([seg_row[:, 1:], seg_row[:, row_count - 1 :]], axis=1)
    after_col = jnp.transpose(jnp.broadcast_to(after, square))
    row_reward = jnp.sum(reward, axis=1, keepdims=True)
    kept = jnp.where(seg_col != after_col, row_reward, 0.0)
    label = lax.broadcasted_iota(jnp.int32, square, 1)
    by_seg = jnp.sum(jnp.where(seg_col == label, kept, 0.0), axis=0, keepdims=True)
    hist = jnp.zeros((1, BINS), jnp.float32)
    last_bin = jnp.zeros((1, BINS), jnp.float32)
    last_seg = seg_row[:, row_count - 1 :]
    for seg in range(SEGS):
        bin_of = bin_ref[seg : seg + 1, :]
        hist = hist + bin_of * by_seg[:, seg : seg + 1]
        last_bin = last_bin + jnp.where(last_seg == seg, bin_of, 0.0)
    bin_id = lax.broadcasted_iota(jnp.int32, (1, BINS), 1).astype(jnp.float32)
    last_bin = jnp.sum(last_bin * bin_id, axis=1, keepdims=True)
    lane = lax.broadcasted_iota(jnp.int32, (1, HD), 1)
    notes = jnp.where(lane == 0, row_reward[row_count - 1 :, :], 0.0)
    notes = notes + jnp.where(lane == 1, last_bin, 0.0)
    notes = notes + jnp.where(lane == 2, seg_row[:, :1].astype(jnp.float32), 0.0)
    notes = notes + jnp.where(lane == 3, last_seg.astype(jnp.float32), 0.0)
    hist_ref[...] = jnp.broadcast_to(jnp.concatenate([hist, notes], axis=1), hist_ref.shape)


def total_kernel(ctx_count, rows_ref, out_ref):
    device_count = rows_ref.shape[0]
    notes = rows_ref[:, BINS:]
    reward, bin_of, first, last = (notes[:, k : k + 1] for k in range(4))
    following = jnp.concatenate([first[1:], first[:1]], axis=0)
    device = lax.broadcasted_iota(jnp.int32, (device_count, 1), 0)
    ends = (following != last) | (lax.rem(device, ctx_count) == ctx_count - 1)
    bin_id = lax.broadcasted_iota(jnp.int32, (device_count, BINS), 1).astype(jnp.float32)
    extra = jnp.where((bin_id == bin_of) & ends, reward, 0.0)
    out_ref[...] = jnp.sum(rows_ref[:, :BINS] + extra, axis=0, keepdims=True)


def local(roll_query, roll_keys, roll_values, pack_dest, segment_ids, reward_bins, reward_weight):
    dp_count = lax.axis_size("dp")
    ctx_count = lax.axis_size("ctx")
    row_count = roll_query.shape[1]
    q_width = roll_query.shape[2]
    kv_width = roll_keys.shape[2]
    block_count = row_count // BLK
    cap = (block_count + dp_count - 1) // dp_count
    slot_count = dp_count * cap
    piece_count = dp_count // 2
    reach = row_count * ctx_count // 2
    hop_count = min(ctx_count - 1, (reach - 1 + row_count - 1) // row_count)
    device_count = dp_count * ctx_count
    smem = pl.BlockSpec(memory_space=pltpu.SMEM)
    vmem = pl.BlockSpec(memory_space=pltpu.VMEM)
    hbm = pl.BlockSpec(memory_space=pl.ANY)

    def across(array, distance):
        return lax.ppermute(array, "dp", [(i, i ^ distance) for i in range(dp_count)])

    half = jax.ShapeDtypeStruct((piece_count * cap, BLK, q_width), jnp.bfloat16)
    sorted_kv, same_query, other_query = pl.pallas_call(
        lambda *refs: sort_kernel(cap, piece_count, *refs),
        out_shape=[jax.ShapeDtypeStruct((slot_count, BLK, 2 * kv_width), jnp.bfloat16), half, half],
        in_specs=[hbm] * 4,
        out_specs=[hbm] * 3,
        scratch_shapes=[
            pltpu.SMEM((dp_count, block_count), jnp.int32),
            pltpu.SMEM((slot_count,), jnp.int32),
            pltpu.SMEM((dp_count,), jnp.int32),
            pltpu.SMEM((slot_count,), jnp.int32),
            pltpu.VMEM((block_count, BLK, kv_width), jnp.bfloat16),
            pltpu.VMEM((block_count, BLK, kv_width), jnp.bfloat16),
            pltpu.VMEM((block_count, BLK, q_width), jnp.bfloat16),
            pltpu.VMEM((slot_count, BLK, 2 * kv_width), jnp.bfloat16),
            pltpu.SemaphoreType.DMA((4,)),
            pltpu.SemaphoreType.DMA((slot_count + 1,)),
        ],
        compiler_params=params(60),
        name="sort",
    )(
        pack_dest,
        roll_keys.reshape(block_count, BLK, kv_width),
        roll_values.reshape(block_count, BLK, kv_width),
        roll_query.reshape(block_count, BLK, q_width),
    )
    got_kv = lax.all_to_all(
        sorted_kv.reshape(dp_count, cap * BLK, 2 * kv_width), "dp", split_axis=0, concat_axis=0, tiled=True
    ).reshape(slot_count, BLK, 2 * kv_width)

    pieces = pl.pallas_call(
        lambda *refs: merge_query_kernel(cap, piece_count, *refs),
        out_shape=[jax.ShapeDtypeStruct((2 * cap, BLK, q_width), jnp.bfloat16)] * piece_count,
        in_specs=[vmem] * 2,
        out_specs=[vmem] * piece_count,
        compiler_params=params(16),
        name="merge_query",
    )(same_query, across(other_query, 1))
    got_query = [pieces[0]] + [across(pieces[i], 2 * i) for i in range(1, piece_count)]
    query = pl.pallas_call(
        lambda *refs: unsort_query_kernel(cap, piece_count, *refs),
        out_shape=jax.ShapeDtypeStruct((block_count, BLK, q_width), jnp.bfloat16),
        in_specs=[smem] + [vmem] * piece_count,
        out_specs=vmem,
        scratch_shapes=[pltpu.SMEM((slot_count,), jnp.int32)],
        compiler_params=params(16),
        name="unsort_query",
    )(pack_dest, *got_query)

    own = pl.pallas_call(
        lambda *refs: unsort_kv_kernel(cap, *refs),
        out_shape=[
            jax.ShapeDtypeStruct((block_count + (share == 0), BLK, 2 * groups * HD), jnp.bfloat16)
            for share, groups in enumerate(SHARES)
        ],
        in_specs=[smem, vmem, vmem],
        out_specs=[vmem] * len(SHARES),
        scratch_shapes=[pltpu.SMEM((slot_count,), jnp.int32)],
        compiler_params=params(16),
        cost_estimate=cost(23000000000, 0),
        name="unsort_kv",
    )(pack_dest, segment_ids, got_kv)
    parts = [own]
    forward = [(i, i + 1) for i in range(ctx_count - 1)]
    for _ in range(hop_count):
        arrays = list(parts[-1])
        if len(parts) == hop_count:
            arrays[-1] = pl.pallas_call(
                after_kernel,
                out_shape=jax.ShapeDtypeStruct(arrays[-1].shape, arrays[-1].dtype),
                in_specs=[hbm] * (1 + (piece_count - 1)),
                out_specs=hbm,
                input_output_aliases={0: 0},
                compiler_params=params(1),
                name="after_query",
            )(arrays[-1], *got_query[1:])
        parts.append([lax.ppermute(array, "ctx", forward) for array in arrays])

    weight_row = reward_weight.reshape(1, q_width)
    out_shape = jax.ShapeDtypeStruct((row_count, q_width), jnp.bfloat16)
    part_count = len(parts)
    first_width, last_width = (groups * GROUP * HD for groups in SHARES)
    attended, reward, bias, bin_of = pl.pallas_call(
        first_kernel,
        grid=(1,),
        out_shape=(
            out_shape,
            jax.ShapeDtypeStruct((row_count, HD), jnp.float32),
            jax.ShapeDtypeStruct((part_count * row_count, row_count), jnp.float32),
            jax.ShapeDtypeStruct((SEGS, BINS), jnp.float32),
        ),
        in_specs=[smem] + [vmem] * (3 + part_count),
        out_specs=(pl.BlockSpec((row_count, first_width), lambda i: (0, 0)), vmem, vmem, vmem),
        compiler_params=params(16),
        name="first_share",
    )(reward_bins, segment_ids, weight_row, query, *[part[0] for part in parts])
    attended, hist_rows = pl.pallas_call(
        last_kernel,
        grid=(1,),
        out_shape=(out_shape, jax.ShapeDtypeStruct((device_count, BINS + HD), jnp.float32)),
        in_specs=[vmem] * 3 + [hbm] + [vmem] * (3 + part_count),
        out_specs=(
            pl.BlockSpec((row_count, last_width), lambda i: (0, first_width // last_width)),
            vmem,
        ),
        input_output_aliases={3: 0},
        compiler_params=params(16),
        name="last_share",
    )(segment_ids, weight_row, query, attended, reward, bias, bin_of, *[part[1] for part in parts])
    gathered = lax.all_to_all(hist_rows, ("dp", "ctx"), split_axis=0, concat_axis=0, tiled=True)
    total = pl.pallas_call(
        lambda *refs: total_kernel(ctx_count, *refs),
        out_shape=jax.ShapeDtypeStruct((1, BINS), jnp.float32),
        in_specs=[vmem],
        out_specs=vmem,
        compiler_params=params(16),
        name="total",
    )(gathered)
    return attended.reshape(1, row_count, q_width), total.reshape(BINS)


def solution(mesh):
    in_specs = (
        P("dp", "ctx", None),
        P("dp", "ctx", None),
        P("dp", "ctx", None),
        P(None, "ctx"),
        P("dp", "ctx"),
        P("dp", None),
        P(),
    )
    out_specs = (P("dp", "ctx", None), P())
    return jax.shard_map(local, mesh=mesh, in_specs=in_specs, out_specs=out_specs, check_vma=False)
```

```python
import math

import jax
import jax.numpy as jnp
from jax import lax
from jax.experimental import pallas as pl
from jax.experimental.pallas import tpu as pltpu
from jax.sharding import PartitionSpec as P

HQ = 32
HK = 4
HD = 128
GROUP = HQ // HK
BLK = 8
SEGS = 16
BINS = 512
NEG = -1e30
SHARES = (2, HK - 2)
FACTOR = math.log2(math.e) / math.sqrt(HD)


def params(mebibytes):
    return pltpu.CompilerParams(vmem_limit_bytes=mebibytes * 1024 * 1024)


def cost(flops, nbytes):
    return pl.CostEstimate(flops=flops, bytes_accessed=nbytes, transcendentals=0)


def find_blocks(dest_ref, block_ref, count_ref, cap, relative):
    dp_count, block_count = dest_ref.shape
    me = lax.axis_index("dp")
    for target in range(dp_count):
        count_ref[target] = 0
    for block in range(block_count):
        target = dest_ref[me, block]
        rank = count_ref[target]
        count_ref[target] = rank + 1
        place = (target ^ me) if relative else target
        block_ref[place * cap + rank] = block


def find_columns(dest_ref, column_ref, cap, relative):
    dp_count, block_count = dest_ref.shape
    me = lax.axis_index("dp")

    def source(src, _):
        place = (src ^ me) if relative else src
        rank = 0
        for block in range(block_count):
            hit = dest_ref[src, block] == me

            @pl.when(hit)
            def _():
                column_ref[place * cap + rank] = block

            rank = rank + jnp.where(hit, 1, 0)
        return 0

    lax.fori_loop(0, dp_count, source, 0)


def sort_kernel(cap, piece_count, dest_hbm, key_hbm, value_hbm, query_hbm, kv_hbm, same_hbm, other_hbm, *scratch):
    dest_ref, block_ref, count_ref, place_ref, key_ref, value_ref, query_ref, stage_ref, in_sem, out_sem = scratch
    arrivals = [
        pltpu.make_async_copy(source, target, in_sem.at[index])
        for index, (source, target) in enumerate(
            ((dest_hbm, dest_ref), (key_hbm, key_ref), (value_hbm, value_ref), (query_hbm, query_ref))
        )
    ]
    for arrival in arrivals:
        arrival.start()
    arrivals[0].wait()
    find_blocks(dest_ref, block_ref, count_ref, cap, False)
    find_blocks(dest_ref, place_ref, count_ref, cap, True)
    arrivals[1].wait()
    arrivals[2].wait()
    width = key_ref.shape[2]
    slot_count = kv_hbm.shape[0]
    for slot in range(slot_count):
        block = block_ref[slot]
        stage_ref[slot, :, :width] = key_ref[block]
        stage_ref[slot, :, width:] = value_ref[block]
    departures = [pltpu.make_async_copy(stage_ref, kv_hbm, out_sem.at[slot_count])]
    departures[0].start()
    arrivals[3].wait()
    for odd, out in ((1, other_hbm), (0, same_hbm)):
        for place in range(piece_count * cap):
            slot = (2 * (place // cap) + odd) * cap + place % cap
            departure = pltpu.make_async_copy(query_ref.at[place_ref[slot]], out.at[place], out_sem.at[slot])
            departure.start()
            departures.append(departure)
    for departure in departures:
        departure.wait()


def merge_query_kernel(cap, piece_count, same_ref, other_ref, *pieces):
    for piece in range(piece_count):
        rows = slice(piece * cap, (piece + 1) * cap)
        pieces[piece][:cap] = same_ref[rows]
        pieces[piece][cap:] = other_ref[rows]


def unsort_query_kernel(cap, piece_count, dest_ref, *rest):
    pieces = rest[:piece_count]
    out_ref, column_ref = rest[piece_count:]
    find_columns(dest_ref, column_ref, cap, True)
    for piece in range(piece_count):
        for place in range(2 * cap):
            out_ref[column_ref[2 * piece * cap + place]] = pieces[piece][place]


def unsort_kv_kernel(cap, dest_ref, bins_ref, seg_ref, got_ref, *rest):
    outs, (bin_ref, column_ref) = rest[:-2], rest[-2:]
    find_columns(dest_ref, column_ref, cap, False)
    lane = lax.broadcasted_iota(jnp.int32, (1, bin_ref.shape[1]), 1)
    for seg in range(SEGS):
        bin_ref[seg : seg + 1, :] = jnp.where(lane == bins_ref[0, seg], 1.0, 0.0)
    block_count = got_ref.shape[0]
    for slot in range(block_count):
        column = column_ref[slot]
        first = 0
        for out_ref, groups in zip(outs, SHARES):
            width = groups * HD
            for half in range(2):
                start = half * HK * HD + first
                out_ref[column, :, half * width : (half + 1) * width] = got_ref[slot, :, start : start + width]
            first += width
    labels = seg_ref[...].astype(jnp.float32)
    labels = jnp.concatenate([labels] * (outs[0].shape[2] // labels.shape[1]), axis=1)
    outs[0][block_count] = jnp.broadcast_to(labels, outs[0].shape[1:]).astype(outs[0].dtype)


def after_kernel(*refs):
    pass


def rows_of(ref, block_count, lane):
    return ref[:block_count, :, lane : lane + HD].reshape(block_count * BLK, HD)


def allowed_bias(label_ref, hop, seg_row):
    row_count = seg_row.shape[1]
    square = (row_count, row_count)
    labels = label_ref[label_ref.shape[0] - 1][:1, :row_count].astype(jnp.float32)
    labels = jnp.transpose(jnp.broadcast_to(labels, square))
    allowed = labels == seg_row.astype(jnp.float32)
    if hop == 0:
        key_pos = lax.broadcasted_iota(jnp.int32, square, 0)
        query_pos = lax.broadcasted_iota(jnp.int32, square, 1)
        allowed = allowed & (key_pos <= query_pos)
    else:
        allowed = allowed & (lax.axis_index("ctx") >= hop)
    return jnp.where(allowed, 0.0, NEG)


def score(keys, query_ref, head):
    here = slice(head * HD, (head + 1) * HD)
    query = query_ref[:, :, here].reshape(query_ref.shape[0] * BLK, HD)
    return lax.dot_general(keys, query, (((1,), (1,)), ((), ())), preferred_element_type=jnp.float32)


def attend_share(share, query_ref, parts, out_ref, bias_ref):
    before = sum(SHARES[:share])
    for index in range(SHARES[share]):
        keys, values = keys_and_values(share, index, query_ref.shape[0], parts)
        heads = range((before + index) * GROUP, (before + index + 1) * GROUP)
        scores = [score(keys, query_ref, head) for head in heads]
        mixed = attend_rows(scores, [values] * GROUP, bias_ref[...])
        attended = [jnp.transpose(each) for each in mixed]
        for head, each in zip(heads, attended):
            first = (head - before * GROUP) * HD
            out_ref[:, first : first + HD] = each


def keys_and_values(share, index, block_count, parts):
    lane = index * HD
    keys = jnp.concatenate([rows_of(part, block_count, lane) for part in parts], axis=0)
    lane = (SHARES[share] + index) * HD
    values = jnp.concatenate([rows_of(part, block_count, lane) for part in parts], axis=0)
    return keys, jnp.transpose(values)


def attend_rows(scores, values, bias):
    scores = [each + bias for each in scores]
    tops = [jnp.max(each, axis=0, keepdims=True) for each in scores]
    weights = [jnp.exp2((each - top) * FACTOR) for each, top in zip(scores, tops)]
    totals = [jnp.sum(each, axis=0, keepdims=True) for each in weights]
    mixed = [
        jnp.dot(value, each.astype(jnp.bfloat16), preferred_element_type=jnp.float32)
        for value, each in zip(values, weights)
    ]
    return [(each * (1.0 / total)).astype(jnp.bfloat16) for each, total in zip(mixed, totals)]


def last_rows(seg_row):
    row_count = seg_row.shape[1]
    position = lax.broadcasted_iota(jnp.int32, (1, row_count), 1)
    after = jnp.concatenate([seg_row[:, 1:], seg_row[:, :1]], axis=1)
    is_last = (after != seg_row) | (position == row_count - 1)
    seg = lax.broadcasted_iota(jnp.int32, (GROUP * SEGS, row_count), 0) % SEGS
    return jnp.where((seg_row == seg) & is_last, 1.0, 0.0).astype(jnp.bfloat16)


def end_rewards(share, end_query_ref, end_bias_ref, end_weight_ref, parts, block_count):
    before = sum(SHARES[:share])
    groups = range(before, before + SHARES[share])
    held = [keys_and_values(share, group - before, block_count, parts) for group in groups]
    scores = [
        lax.dot_general(
            keys, end_query_ref[group], (((1,), (1,)), ((), ())), preferred_element_type=jnp.float32
        )
        for group, (keys, _) in zip(groups, held)
    ]
    attended = attend_rows(scores, [values for _, values in held], end_bias_ref[...])
    products = [each.astype(jnp.float32) * end_weight_ref[group] for group, each in zip(groups, attended)]
    return sum(jnp.sum(each, axis=0, keepdims=True) for each in products)


def first_kernel(seg_ref, weight_ref, query_ref, *rest):
    parts, rest = rest[:-6], rest[-6:]
    out_ref, bias_ref, end_query_ref, end_bias_ref, end_weight_ref, reward_ref = rest
    row_count = seg_ref.shape[1]
    block_count = query_ref.shape[0]
    for hop, part in enumerate(parts):
        bias_ref[hop * row_count : (hop + 1) * row_count, :] = allowed_bias(part, hop, seg_ref[...])
    chosen = last_rows(seg_ref[...])
    end_bias_ref[...] = lax.dot_general(
        bias_ref[...].astype(jnp.bfloat16),
        chosen,
        (((1,), (1,)), ((), ())),
        preferred_element_type=jnp.float32,
    )
    for group in range(HK):
        rows, weights = [], []
        for head in range(group * GROUP, (group + 1) * GROUP):
            here = slice(head * HD, (head + 1) * HD)
            query = query_ref[:, :, here].reshape(row_count, HD)
            rows.append(jnp.dot(chosen[:SEGS], query, preferred_element_type=jnp.float32))
            weights.append(jnp.broadcast_to(weight_ref[:, here], (SEGS, HD)))
        end_query_ref[group] = jnp.concatenate(rows, axis=0).astype(jnp.bfloat16)
        end_weight_ref[group] = jnp.transpose(jnp.concatenate(weights, axis=0))
    reward_ref[...] = end_rewards(0, end_query_ref, end_bias_ref, end_weight_ref, parts, block_count)
    attend_share(0, query_ref, parts, out_ref, bias_ref)


def ends_kernel(seg_ref, end_query_ref, end_bias_ref, end_weight_ref, reward_ref, bin_ref, *rest):
    parts, hist_ref = rest[:-1], rest[-1]
    seg_row = seg_ref[...]
    row_count = seg_row.shape[1]
    block_count = row_count // BLK
    reward = reward_ref[...] + end_rewards(
        1, end_query_ref, end_bias_ref, end_weight_ref, parts, block_count
    )
    ends = reward.shape[1]
    by_seg = jnp.transpose(jnp.broadcast_to(reward, (ends, ends)))
    by_seg = jnp.sum(by_seg.reshape(GROUP, SEGS, ends), axis=0)
    seg = lax.broadcasted_iota(jnp.int32, (SEGS, ends), 0)
    first_seg, last_seg = seg_row[:, :1], seg_row[:, row_count - 1 :]
    seg_rows = jnp.broadcast_to(seg_row, (SEGS, row_count))
    row_seg = lax.broadcasted_iota(jnp.int32, seg_rows.shape, 0)
    present = jnp.max(jnp.where(seg_rows == row_seg, 1, 0), axis=1, keepdims=True)
    certain = jnp.where((present > 0) & (seg != last_seg), by_seg, 0.0)
    bin_of = bin_ref[...]
    hist = jnp.sum(bin_of * jnp.concatenate([certain] * (BINS // ends), axis=1), axis=0, keepdims=True)
    last_reward = jnp.sum(jnp.where(seg == last_seg, by_seg, 0.0), axis=0, keepdims=True)
    bin_id = lax.broadcasted_iota(jnp.int32, (SEGS, BINS), 1).astype(jnp.float32)
    row_id = lax.broadcasted_iota(jnp.int32, (SEGS, BINS), 0)
    last_bin = jnp.where(row_id == last_seg, bin_of * bin_id, 0.0)
    last_bin = jnp.sum(jnp.sum(last_bin, axis=0, keepdims=True), axis=1, keepdims=True)
    lane = lax.broadcasted_iota(jnp.int32, (1, HD), 1)
    notes = jnp.where(lane == 0, last_reward, 0.0)
    notes = notes + jnp.where(lane == 1, last_bin, 0.0)
    notes = notes + jnp.where(lane == 2, first_seg.astype(jnp.float32), 0.0)
    notes = notes + jnp.where(lane == 3, last_seg.astype(jnp.float32), 0.0)
    row = jnp.concatenate([hist, notes], axis=1)
    hist_ref[...] = jnp.broadcast_to(row.reshape(1, 1, row.shape[1]), hist_ref.shape)


def last_kernel(query_ref, before_ref, bias_ref, *rest):
    attend_share(1, query_ref, rest[:-1], rest[-1], bias_ref)


def total_kernel(ctx_count, rows_ref, out_ref):
    device_count = rows_ref.shape[0]
    rows = rows_ref[...].reshape(device_count, rows_ref.shape[2])
    notes = rows[:, BINS:]
    reward, bin_of, first, last = (notes[:, k : k + 1] for k in range(4))
    following = jnp.concatenate([first[1:], first[:1]], axis=0)
    device = lax.broadcasted_iota(jnp.int32, (device_count, 1), 0)
    ends = (following != last) | (lax.rem(device, ctx_count) == ctx_count - 1)
    bin_id = lax.broadcasted_iota(jnp.int32, (device_count, BINS), 1).astype(jnp.float32)
    extra = jnp.where((bin_id == bin_of) & ends, reward, 0.0)
    out_ref[...] = jnp.sum(rows[:, :BINS] + extra, axis=0, keepdims=True)


def local(roll_query, roll_keys, roll_values, pack_dest, segment_ids, reward_bins, reward_weight):
    dp_count = lax.axis_size("dp")
    ctx_count = lax.axis_size("ctx")
    row_count = roll_query.shape[1]
    q_width = roll_query.shape[2]
    kv_width = roll_keys.shape[2]
    block_count = row_count // BLK
    cap = (block_count + dp_count - 1) // dp_count
    slot_count = dp_count * cap
    piece_count = dp_count // 2
    reach = row_count * ctx_count // 2
    hop_count = min(ctx_count - 1, (reach - 1 + row_count - 1) // row_count)
    device_count = dp_count * ctx_count
    smem = pl.BlockSpec(memory_space=pltpu.SMEM)
    vmem = pl.BlockSpec(memory_space=pltpu.VMEM)
    hbm = pl.BlockSpec(memory_space=pl.ANY)

    def across(array, distance):
        return lax.ppermute(array, "dp", [(i, i ^ distance) for i in range(dp_count)])

    half = jax.ShapeDtypeStruct((piece_count * cap, BLK, q_width), jnp.bfloat16)
    sorted_kv, same_query, other_query = pl.pallas_call(
        lambda *refs: sort_kernel(cap, piece_count, *refs),
        out_shape=[jax.ShapeDtypeStruct((slot_count, BLK, 2 * kv_width), jnp.bfloat16), half, half],
        in_specs=[hbm] * 4,
        out_specs=[hbm] * 3,
        scratch_shapes=[
            pltpu.SMEM((dp_count, block_count), jnp.int32),
            pltpu.SMEM((slot_count,), jnp.int32),
            pltpu.SMEM((dp_count,), jnp.int32),
            pltpu.SMEM((slot_count,), jnp.int32),
            pltpu.VMEM((block_count, BLK, kv_width), jnp.bfloat16),
            pltpu.VMEM((block_count, BLK, kv_width), jnp.bfloat16),
            pltpu.VMEM((block_count, BLK, q_width), jnp.bfloat16),
            pltpu.VMEM((slot_count, BLK, 2 * kv_width), jnp.bfloat16),
            pltpu.SemaphoreType.DMA((4,)),
            pltpu.SemaphoreType.DMA((slot_count + 1,)),
        ],
        compiler_params=params(60),
        name="sort",
    )(
        pack_dest,
        roll_keys.reshape(block_count, BLK, kv_width),
        roll_values.reshape(block_count, BLK, kv_width),
        roll_query.reshape(block_count, BLK, q_width),
    )
    got_kv = lax.all_to_all(
        sorted_kv.reshape(dp_count, cap * BLK, 2 * kv_width), "dp", split_axis=0, concat_axis=0, tiled=True
    ).reshape(slot_count, BLK, 2 * kv_width)

    pieces = pl.pallas_call(
        lambda *refs: merge_query_kernel(cap, piece_count, *refs),
        out_shape=[jax.ShapeDtypeStruct((2 * cap, BLK, q_width), jnp.bfloat16)] * piece_count,
        in_specs=[vmem] * 2,
        out_specs=[vmem] * piece_count,
        compiler_params=params(16),
        name="merge_query",
    )(same_query, across(other_query, 1))
    got_query = [pieces[0]] + [across(pieces[i], 2 * i) for i in range(1, piece_count)]
    query = pl.pallas_call(
        lambda *refs: unsort_query_kernel(cap, piece_count, *refs),
        out_shape=jax.ShapeDtypeStruct((block_count, BLK, q_width), jnp.bfloat16),
        in_specs=[smem] + [vmem] * piece_count,
        out_specs=vmem,
        scratch_shapes=[pltpu.SMEM((slot_count,), jnp.int32)],
        compiler_params=params(16),
        name="unsort_query",
    )(pack_dest, *got_query)

    *own, bin_of = pl.pallas_call(
        lambda *refs: unsort_kv_kernel(cap, *refs),
        out_shape=[
            jax.ShapeDtypeStruct((block_count + (share == 0), BLK, 2 * groups * HD), jnp.bfloat16)
            for share, groups in enumerate(SHARES)
        ]
        + [jax.ShapeDtypeStruct((SEGS, BINS), jnp.float32)],
        in_specs=[smem, smem, vmem, vmem],
        out_specs=[vmem] * (len(SHARES) + 1),
        scratch_shapes=[pltpu.SMEM((slot_count,), jnp.int32)],
        compiler_params=params(16),
        cost_estimate=cost(23000000000, 0),
        name="unsort_kv",
    )(pack_dest, reward_bins, segment_ids, got_kv)
    parts = [own]
    forward = [(i, i + 1) for i in range(ctx_count - 1)]
    for _ in range(hop_count):
        arrays = list(parts[-1])
        if len(parts) == hop_count:
            arrays[-1] = pl.pallas_call(
                after_kernel,
                out_shape=jax.ShapeDtypeStruct(arrays[-1].shape, arrays[-1].dtype),
                in_specs=[hbm] * 2,
                out_specs=hbm,
                input_output_aliases={0: 0},
                compiler_params=params(1),
                name="after_query",
            )(arrays[-1], query)
        parts.append([lax.ppermute(array, "ctx", forward) for array in arrays])

    weight_row = reward_weight.reshape(1, q_width)
    out_shape = jax.ShapeDtypeStruct((row_count, q_width), jnp.bfloat16)
    part_count = len(parts)
    first_width, last_width = (groups * GROUP * HD for groups in SHARES)
    ends = GROUP * SEGS
    attended, bias, *end_state = pl.pallas_call(
        first_kernel,
        grid=(1,),
        out_shape=(
            out_shape,
            jax.ShapeDtypeStruct((part_count * row_count, row_count), jnp.float32),
            jax.ShapeDtypeStruct((HK, ends, HD), jnp.bfloat16),
            jax.ShapeDtypeStruct((part_count * row_count, ends), jnp.float32),
            jax.ShapeDtypeStruct((HK, HD, ends), jnp.float32),
            jax.ShapeDtypeStruct((1, ends), jnp.float32),
        ),
        in_specs=[vmem] * (3 + part_count),
        out_specs=(pl.BlockSpec((row_count, first_width), lambda i: (0, 0)),) + (vmem,) * 5,
        compiler_params=params(16),
        name="first_share",
    )(segment_ids, weight_row, query, *[part[0] for part in parts])
    hist_rows = pl.pallas_call(
        ends_kernel,
        out_shape=jax.ShapeDtypeStruct((device_count, 1, BINS + HD), jnp.float32),
        in_specs=[vmem] * (6 + part_count),
        out_specs=vmem,
        compiler_params=params(16),
        name="ends",
    )(segment_ids, *end_state, bin_of, *[part[1] for part in parts])
    attended = pl.pallas_call(
        last_kernel,
        grid=(1,),
        out_shape=out_shape,
        in_specs=[vmem, hbm] + [vmem] * (1 + part_count),
        out_specs=pl.BlockSpec((row_count, last_width), lambda i: (0, first_width // last_width)),
        input_output_aliases={1: 0},
        compiler_params=params(16),
        name="last_share",
    )(query, attended, bias, *[part[1] for part in parts])
    gathered = lax.all_to_all(hist_rows, ("dp", "ctx"), split_axis=0, concat_axis=0, tiled=True)
    total = pl.pallas_call(
        lambda *refs: total_kernel(ctx_count, *refs),
        out_shape=jax.ShapeDtypeStruct((1, BINS), jnp.float32),
        in_specs=[vmem],
        out_specs=vmem,
        compiler_params=params(16),
        name="total",
    )(gathered)
    return attended.reshape(1, row_count, q_width), total.reshape(BINS)


def solution(mesh):
    in_specs = (
        P("dp", "ctx", None),
        P("dp", "ctx", None),
        P("dp", "ctx", None),
        P(None, "ctx"),
        P("dp", "ctx"),
        P("dp", None),
        P(),
    )
    out_specs = (P("dp", "ctx", None), P())
    return jax.shard_map(local, mesh=mesh, in_specs=in_specs, out_specs=out_specs, check_vma=False)
```

```python
import math

import jax
import jax.numpy as jnp
from jax import lax
from jax.experimental import pallas as pl
from jax.experimental.pallas import tpu as pltpu
from jax.sharding import PartitionSpec as P

HQ = 32
HK = 4
HD = 128
GROUP = HQ // HK
BLK = 8
SEGS = 16
BINS = 512
NEG = -1e30
FIRST_LANE, LAST_LANE, BIN_LANE = 2 * SEGS - 2, 2 * SEGS - 1, 2 * SEGS
SHARES = (2, HK - 2)
FACTOR = math.log2(math.e) / math.sqrt(HD)


def params(mebibytes):
    return pltpu.CompilerParams(vmem_limit_bytes=mebibytes * 1024 * 1024)


def cost(flops, nbytes):
    return pl.CostEstimate(flops=flops, bytes_accessed=nbytes, transcendentals=0)


def find_blocks(dest_ref, block_ref, place_ref, count_ref, cap):
    dp_count, block_count = dest_ref.shape
    me = lax.axis_index("dp")
    for target in range(dp_count):
        count_ref[target] = 0
    for block in range(block_count):
        target = dest_ref[me, block]
        rank = count_ref[target]
        count_ref[target] = rank + 1
        block_ref[target * cap + rank] = block
        place_ref[(target ^ me) * cap + rank] = block


def find_columns(dest_ref, column_ref, cap, relative):
    dp_count, block_count = dest_ref.shape
    me = lax.axis_index("dp")

    def source(src, _):
        place = (src ^ me) if relative else src
        rank = 0
        for block in range(block_count):
            hit = dest_ref[src, block] == me

            @pl.when(hit)
            def _():
                column_ref[place * cap + rank] = block

            rank = rank + jnp.where(hit, 1, 0)
        return 0

    lax.fori_loop(0, dp_count, source, 0)


def sort_kernel(cap, piece_count, dest_hbm, key_hbm, value_hbm, query_hbm, kv_hbm, same_hbm, other_hbm, *scratch):
    dest_ref, block_ref, count_ref, place_ref, key_ref, value_ref, query_ref, stage_ref, in_sem, out_sem = scratch
    arrivals = [
        pltpu.make_async_copy(source, target, in_sem.at[index])
        for index, (source, target) in enumerate(
            ((dest_hbm, dest_ref), (key_hbm, key_ref), (value_hbm, value_ref), (query_hbm, query_ref))
        )
    ]
    for arrival in arrivals:
        arrival.start()
    arrivals[0].wait()
    find_blocks(dest_ref, block_ref, place_ref, count_ref, cap)
    arrivals[1].wait()
    arrivals[2].wait()
    width = key_ref.shape[2]
    slot_count = kv_hbm.shape[0]
    for slot in range(slot_count):
        block = block_ref[slot]
        stage_ref[slot, :, :width] = key_ref[block]
        stage_ref[slot, :, width:] = value_ref[block]
    departures = [pltpu.make_async_copy(stage_ref, kv_hbm, out_sem.at[slot_count])]
    departures[0].start()
    arrivals[3].wait()
    for odd, out in ((1, other_hbm), (0, same_hbm)):
        for place in range(piece_count * cap):
            slot = (2 * (place // cap) + odd) * cap + place % cap
            departure = pltpu.make_async_copy(query_ref.at[place_ref[slot]], out.at[place], out_sem.at[slot])
            departure.start()
            departures.append(departure)
    for departure in departures:
        departure.wait()


def merge_query_kernel(cap, piece_count, same_ref, other_ref, *pieces):
    for piece in range(piece_count):
        rows = slice(piece * cap, (piece + 1) * cap)
        pieces[piece][:cap] = same_ref[rows]
        pieces[piece][cap:] = other_ref[rows]


def unsort_query_kernel(cap, piece_count, dest_ref, *rest):
    pieces = rest[:piece_count]
    out_ref, column_ref = rest[piece_count:]
    find_columns(dest_ref, column_ref, cap, True)
    for piece in range(piece_count):
        for place in range(2 * cap):
            out_ref[column_ref[2 * piece * cap + place]] = pieces[piece][place]


def unsort_kv_kernel(cap, dest_ref, bins_ref, seg_ref, got_ref, *rest):
    outs, (bin_ref, column_ref) = rest[:-2], rest[-2:]
    find_columns(dest_ref, column_ref, cap, False)
    lane = lax.broadcasted_iota(jnp.int32, (1, HD), 1)
    bins = jnp.zeros((1, HD), jnp.int32)
    for seg in range(SEGS):
        bins = jnp.where(lane == BIN_LANE + seg, bins_ref[0, seg], bins)
    bin_ref[...] = bins.astype(jnp.float32)
    block_count = got_ref.shape[0]
    for slot in range(block_count):
        column = column_ref[slot]
        first = 0
        for out_ref, groups in zip(outs, SHARES):
            width = groups * HD
            for half in range(2):
                start = half * HK * HD + first
                out_ref[column, :, half * width : (half + 1) * width] = got_ref[slot, :, start : start + width]
            first += width
    labels = seg_ref[...].astype(jnp.float32)
    labels = jnp.concatenate([labels] * (outs[0].shape[2] // labels.shape[1]), axis=1)
    outs[0][block_count] = jnp.broadcast_to(labels, outs[0].shape[1:]).astype(outs[0].dtype)


def after_kernel(*refs):
    pass


def rows_of(ref, block_count, lane):
    return ref[:block_count, :, lane : lane + HD].reshape(block_count * BLK, HD)


def allowed_bias(label_ref, hop, seg_row):
    row_count = seg_row.shape[1]
    square = (row_count, row_count)
    labels = label_ref[label_ref.shape[0] - 1][:1, :row_count].astype(jnp.float32)
    labels = jnp.transpose(jnp.broadcast_to(labels, square))
    allowed = labels == seg_row.astype(jnp.float32)
    if hop == 0:
        key_pos = lax.broadcasted_iota(jnp.int32, square, 0)
        query_pos = lax.broadcasted_iota(jnp.int32, square, 1)
        allowed = allowed & (key_pos <= query_pos)
    else:
        allowed = allowed & (lax.axis_index("ctx") >= hop)
    return jnp.where(allowed, 0.0, NEG)


def score(keys, query_ref, head):
    here = slice(head * HD, (head + 1) * HD)
    query = query_ref[:, :, here].reshape(query_ref.shape[0] * BLK, HD)
    return lax.dot_general(keys, query, (((1,), (1,)), ((), ())), preferred_element_type=jnp.float32)


def attend_share(share, query_ref, parts, out_ref, bias_ref):
    before = sum(SHARES[:share])
    for index in range(SHARES[share]):
        keys, values = keys_and_values(share, index, query_ref.shape[0], parts)
        heads = range((before + index) * GROUP, (before + index + 1) * GROUP)
        scores = [score(keys, query_ref, head) for head in heads]
        mixed = attend_rows(scores, [values] * GROUP, bias_ref[...])
        attended = [jnp.transpose(each) for each in mixed]
        for head, each in zip(heads, attended):
            first = (head - before * GROUP) * HD
            out_ref[:, first : first + HD] = each


def keys_and_values(share, index, block_count, parts):
    lane = index * HD
    keys = jnp.concatenate([rows_of(part, block_count, lane) for part in parts], axis=0)
    lane = (SHARES[share] + index) * HD
    values = jnp.concatenate([rows_of(part, block_count, lane) for part in parts], axis=0)
    return keys, jnp.transpose(values)


def attend_rows(scores, values, bias):
    scores = [each + bias for each in scores]
    tops = [jnp.max(each, axis=0, keepdims=True) for each in scores]
    weights = [jnp.exp2((each - top) * FACTOR) for each, top in zip(scores, tops)]
    totals = [jnp.sum(each, axis=0, keepdims=True) for each in weights]
    mixed = [
        jnp.dot(value, each.astype(jnp.bfloat16), preferred_element_type=jnp.float32)
        for value, each in zip(values, weights)
    ]
    return [(each * (1.0 / total)).astype(jnp.bfloat16) for each, total in zip(mixed, totals)]


def last_rows(seg_row):
    row_count = seg_row.shape[1]
    position = lax.broadcasted_iota(jnp.int32, (1, row_count), 1)
    after = jnp.concatenate([seg_row[:, 1:], seg_row[:, :1]], axis=1)
    is_last = (after != seg_row) | (position == row_count - 1)
    seg = lax.broadcasted_iota(jnp.int32, (GROUP * SEGS, row_count), 0) % SEGS
    return jnp.where((seg_row == seg) & is_last, 1.0, 0.0).astype(jnp.bfloat16)


def end_rewards(share, end_query_ref, end_bias_ref, end_weight_ref, parts, block_count):
    before = sum(SHARES[:share])
    groups = range(before, before + SHARES[share])
    held = [keys_and_values(share, group - before, block_count, parts) for group in groups]
    scores = [
        lax.dot_general(
            keys, end_query_ref[group], (((1,), (1,)), ((), ())), preferred_element_type=jnp.float32
        )
        for group, (keys, _) in zip(groups, held)
    ]
    attended = attend_rows(scores, [values for _, values in held], end_bias_ref[...])
    products = [each.astype(jnp.float32) * end_weight_ref[group] for group, each in zip(groups, attended)]
    return sum(jnp.sum(each, axis=0, keepdims=True) for each in products)


def first_kernel(seg_ref, weight_ref, query_ref, *rest):
    parts, rest = rest[:-6], rest[-6:]
    out_ref, bias_ref, end_query_ref, end_bias_ref, end_weight_ref, reward_ref = rest
    row_count = seg_ref.shape[1]
    block_count = query_ref.shape[0]
    for hop, part in enumerate(parts):
        bias_ref[hop * row_count : (hop + 1) * row_count, :] = allowed_bias(part, hop, seg_ref[...])
    chosen = last_rows(seg_ref[...])
    end_bias_ref[...] = lax.dot_general(
        bias_ref[...].astype(jnp.bfloat16),
        chosen,
        (((1,), (1,)), ((), ())),
        preferred_element_type=jnp.float32,
    )
    for group in range(HK):
        rows, weights = [], []
        for head in range(group * GROUP, (group + 1) * GROUP):
            here = slice(head * HD, (head + 1) * HD)
            query = query_ref[:, :, here].reshape(row_count, HD)
            rows.append(jnp.dot(chosen[:SEGS], query, preferred_element_type=jnp.float32))
            weights.append(jnp.broadcast_to(weight_ref[:, here], (SEGS, HD)))
        end_query_ref[group] = jnp.concatenate(rows, axis=0).astype(jnp.bfloat16)
        end_weight_ref[group] = jnp.transpose(jnp.concatenate(weights, axis=0))
    reward_ref[...] = end_rewards(0, end_query_ref, end_bias_ref, end_weight_ref, parts, block_count)
    attend_share(0, query_ref, parts, out_ref, bias_ref)


def ends_kernel(seg_ref, end_query_ref, end_bias_ref, end_weight_ref, reward_ref, bin_ref, *rest):
    parts, hist_ref = rest[:-1], rest[-1]
    seg_row = seg_ref[...]
    row_count = seg_row.shape[1]
    block_count = row_count // BLK
    reward = reward_ref[...] + end_rewards(
        1, end_query_ref, end_bias_ref, end_weight_ref, parts, block_count
    )
    by_seg = reward[:, :SEGS]
    for head in range(1, GROUP):
        by_seg = by_seg + reward[:, head * SEGS : (head + 1) * SEGS]
    by_seg = jnp.concatenate([by_seg, jnp.zeros((1, HD - SEGS), jnp.float32)], axis=1)
    lane = lax.broadcasted_iota(jnp.int32, (1, HD), 1)
    seg_rows = jnp.transpose(jnp.broadcast_to(seg_row, (row_count, row_count)))
    present = jnp.max(jnp.where(seg_rows == lane, 1, 0), axis=0, keepdims=True)
    first_seg, last_seg = seg_row[:, :1], seg_row[:, row_count - 1 :]
    row = bin_ref[...] + jnp.where(present > 0, by_seg, 0.0)
    row = row + jnp.where(lane == FIRST_LANE, first_seg.astype(jnp.float32), 0.0)
    row = row + jnp.where(lane == LAST_LANE, last_seg.astype(jnp.float32), 0.0)
    hist_ref[...] = jnp.broadcast_to(row.reshape(1, 1, HD), hist_ref.shape)


def last_kernel(query_ref, before_ref, bias_ref, *rest):
    attend_share(1, query_ref, rest[:-1], rest[-1], bias_ref)


def total_kernel(ctx_count, rows_ref, out_ref):
    device_count = rows_ref.shape[0]
    rows = rows_ref[...]
    first = rows[:, :, FIRST_LANE : FIRST_LANE + 1]
    last = rows[:, :, LAST_LANE : LAST_LANE + 1]
    following = jnp.concatenate([first[1:], first[:1]], axis=0)
    device = lax.broadcasted_iota(jnp.int32, first.shape, 0)
    ends = (following != last) | (lax.rem(device, ctx_count) == ctx_count - 1)
    lane = lax.broadcasted_iota(jnp.int32, rows.shape, 2)
    kept = (lane < SEGS) & ((lane.astype(jnp.float32) != last) | ends)
    rewards = jnp.where(kept, rows, 0.0)
    groups = (device_count // ctx_count, ctx_count, 1, HD)
    rewards = jnp.sum(rewards.reshape(groups), axis=1).reshape(groups[0], HD)
    bins = rows.reshape(groups)[:, 0].reshape(groups[0], HD)
    bin_id = lax.broadcasted_iota(jnp.int32, (groups[0], BINS), 1).astype(jnp.float32)
    hist = jnp.zeros((groups[0], BINS), jnp.float32)
    for seg in range(SEGS):
        bin_of = bins[:, BIN_LANE + seg : BIN_LANE + seg + 1]
        hist = hist + jnp.where(bin_id == bin_of, rewards[:, seg : seg + 1], 0.0)
    out_ref[...] = jnp.sum(hist, axis=0, keepdims=True)


def local(roll_query, roll_keys, roll_values, pack_dest, segment_ids, reward_bins, reward_weight):
    dp_count = lax.axis_size("dp")
    ctx_count = lax.axis_size("ctx")
    row_count = roll_query.shape[1]
    q_width = roll_query.shape[2]
    kv_width = roll_keys.shape[2]
    block_count = row_count // BLK
    cap = (block_count + dp_count - 1) // dp_count
    slot_count = dp_count * cap
    piece_count = dp_count // 2
    reach = row_count * ctx_count // 2
    hop_count = min(ctx_count - 1, (reach - 1 + row_count - 1) // row_count)
    device_count = dp_count * ctx_count
    smem = pl.BlockSpec(memory_space=pltpu.SMEM)
    vmem = pl.BlockSpec(memory_space=pltpu.VMEM)
    hbm = pl.BlockSpec(memory_space=pl.ANY)

    def across(array, distance):
        return lax.ppermute(array, "dp", [(i, i ^ distance) for i in range(dp_count)])

    half = jax.ShapeDtypeStruct((piece_count * cap, BLK, q_width), jnp.bfloat16)
    sorted_kv, same_query, other_query = pl.pallas_call(
        lambda *refs: sort_kernel(cap, piece_count, *refs),
        out_shape=[jax.ShapeDtypeStruct((slot_count, BLK, 2 * kv_width), jnp.bfloat16), half, half],
        in_specs=[hbm] * 4,
        out_specs=[hbm] * 3,
        scratch_shapes=[
            pltpu.SMEM((dp_count, block_count), jnp.int32),
            pltpu.SMEM((slot_count,), jnp.int32),
            pltpu.SMEM((dp_count,), jnp.int32),
            pltpu.SMEM((slot_count,), jnp.int32),
            pltpu.VMEM((block_count, BLK, kv_width), jnp.bfloat16),
            pltpu.VMEM((block_count, BLK, kv_width), jnp.bfloat16),
            pltpu.VMEM((block_count, BLK, q_width), jnp.bfloat16),
            pltpu.VMEM((slot_count, BLK, 2 * kv_width), jnp.bfloat16),
            pltpu.SemaphoreType.DMA((4,)),
            pltpu.SemaphoreType.DMA((slot_count + 1,)),
        ],
        compiler_params=params(60),
        name="sort",
    )(
        pack_dest,
        roll_keys.reshape(block_count, BLK, kv_width),
        roll_values.reshape(block_count, BLK, kv_width),
        roll_query.reshape(block_count, BLK, q_width),
    )
    got_kv = lax.all_to_all(
        sorted_kv.reshape(dp_count, cap * BLK, 2 * kv_width), "dp", split_axis=0, concat_axis=0, tiled=True
    ).reshape(slot_count, BLK, 2 * kv_width)

    pieces = pl.pallas_call(
        lambda *refs: merge_query_kernel(cap, piece_count, *refs),
        out_shape=[jax.ShapeDtypeStruct((2 * cap, BLK, q_width), jnp.bfloat16)] * piece_count,
        in_specs=[vmem] * 2,
        out_specs=[vmem] * piece_count,
        compiler_params=params(16),
        name="merge_query",
    )(same_query, across(other_query, 1))
    got_query = [pieces[0]] + [across(pieces[i], 2 * i) for i in range(1, piece_count)]
    query = pl.pallas_call(
        lambda *refs: unsort_query_kernel(cap, piece_count, *refs),
        out_shape=jax.ShapeDtypeStruct((block_count, BLK, q_width), jnp.bfloat16),
        in_specs=[smem] + [vmem] * piece_count,
        out_specs=vmem,
        scratch_shapes=[pltpu.SMEM((slot_count,), jnp.int32)],
        compiler_params=params(16),
        name="unsort_query",
    )(pack_dest, *got_query)

    *own, bin_of = pl.pallas_call(
        lambda *refs: unsort_kv_kernel(cap, *refs),
        out_shape=[
            jax.ShapeDtypeStruct((block_count + (share == 0), BLK, 2 * groups * HD), jnp.bfloat16)
            for share, groups in enumerate(SHARES)
        ]
        + [jax.ShapeDtypeStruct((1, HD), jnp.float32)],
        in_specs=[smem, smem, vmem, vmem],
        out_specs=[vmem] * (len(SHARES) + 1),
        scratch_shapes=[pltpu.SMEM((slot_count,), jnp.int32)],
        compiler_params=params(16),
        cost_estimate=cost(23000000000, 0),
        name="unsort_kv",
    )(pack_dest, reward_bins, segment_ids, got_kv)
    parts = [own]
    forward = [(i, i + 1) for i in range(ctx_count - 1)]
    for _ in range(hop_count):
        arrays = list(parts[-1])
        if len(parts) == hop_count:
            arrays[-1] = pl.pallas_call(
                after_kernel,
                out_shape=jax.ShapeDtypeStruct(arrays[-1].shape, arrays[-1].dtype),
                in_specs=[hbm] * 2,
                out_specs=hbm,
                input_output_aliases={0: 0},
                compiler_params=params(1),
                name="after_query",
            )(arrays[-1], query)
        parts.append([lax.ppermute(array, "ctx", forward) for array in arrays])

    weight_row = reward_weight.reshape(1, q_width)
    out_shape = jax.ShapeDtypeStruct((row_count, q_width), jnp.bfloat16)
    part_count = len(parts)
    first_width, last_width = (groups * GROUP * HD for groups in SHARES)
    ends = GROUP * SEGS
    attended, bias, *end_state = pl.pallas_call(
        first_kernel,
        grid=(1,),
        out_shape=(
            out_shape,
            jax.ShapeDtypeStruct((part_count * row_count, row_count), jnp.float32),
            jax.ShapeDtypeStruct((HK, ends, HD), jnp.bfloat16),
            jax.ShapeDtypeStruct((part_count * row_count, ends), jnp.float32),
            jax.ShapeDtypeStruct((HK, HD, ends), jnp.float32),
            jax.ShapeDtypeStruct((1, ends), jnp.float32),
        ),
        in_specs=[vmem] * (3 + part_count),
        out_specs=(pl.BlockSpec((row_count, first_width), lambda i: (0, 0)),) + (vmem,) * 5,
        compiler_params=params(16),
        name="first_share",
    )(segment_ids, weight_row, query, *[part[0] for part in parts])
    hist_rows = pl.pallas_call(
        ends_kernel,
        out_shape=jax.ShapeDtypeStruct((device_count, 1, HD), jnp.float32),
        in_specs=[vmem] * (6 + part_count),
        out_specs=vmem,
        compiler_params=params(16),
        name="ends",
    )(segment_ids, *end_state, bin_of, *[part[1] for part in parts])
    attended = pl.pallas_call(
        last_kernel,
        grid=(1,),
        out_shape=out_shape,
        in_specs=[vmem, hbm] + [vmem] * (1 + part_count),
        out_specs=pl.BlockSpec((row_count, last_width), lambda i: (0, first_width // last_width)),
        input_output_aliases={1: 0},
        compiler_params=params(16),
        name="last_share",
    )(query, attended, bias, *[part[1] for part in parts])
    gathered = lax.all_to_all(hist_rows, ("dp", "ctx"), split_axis=0, concat_axis=0, tiled=True)
    total = pl.pallas_call(
        lambda *refs: total_kernel(ctx_count, *refs),
        out_shape=jax.ShapeDtypeStruct((1, BINS), jnp.float32),
        in_specs=[vmem],
        out_specs=vmem,
        compiler_params=params(16),
        name="total",
    )(gathered)
    return attended.reshape(1, row_count, q_width), total.reshape(BINS)


def solution(mesh):
    in_specs = (
        P("dp", "ctx", None),
        P("dp", "ctx", None),
        P("dp", "ctx", None),
        P(None, "ctx"),
        P("dp", "ctx"),
        P("dp", None),
        P(),
    )
    out_specs = (P("dp", "ctx", None), P())
    return jax.shard_map(local, mesh=mesh, in_specs=in_specs, out_specs=out_specs, check_vma=False)
```

```python
import math

import jax
import jax.numpy as jnp
from jax import lax
from jax.experimental import pallas as pl
from jax.experimental.pallas import tpu as pltpu
from jax.sharding import PartitionSpec as P

HQ = 32
HK = 4
HD = 128
GROUP = HQ // HK
BLK = 8
SEGS = 16
BINS = 512
NEG = -1e30
FIRST_LANE, LAST_LANE, BIN_LANE = 2 * SEGS - 2, 2 * SEGS - 1, 2 * SEGS
SHARES = (2, HK - 2)
FACTOR = math.log2(math.e) / math.sqrt(HD)


def params(mebibytes):
    return pltpu.CompilerParams(vmem_limit_bytes=mebibytes * 1024 * 1024)


def cost(flops, nbytes):
    return pl.CostEstimate(flops=flops, bytes_accessed=nbytes, transcendentals=0)


def find_blocks(dest_ref, block_ref, place_ref, count_ref, cap):
    dp_count, block_count = dest_ref.shape
    me = lax.axis_index("dp")
    for target in range(dp_count):
        count_ref[target] = 0
    for block in range(block_count):
        target = dest_ref[me, block]
        rank = count_ref[target]
        count_ref[target] = rank + 1
        block_ref[target * cap + rank] = block
        place_ref[(target ^ me) * cap + rank] = block


def find_columns(dest_ref, column_ref, cap, relative):
    dp_count, block_count = dest_ref.shape
    me = lax.axis_index("dp")

    def source(src, _):
        place = (src ^ me) if relative else src
        rank = 0
        for block in range(block_count):
            hit = dest_ref[src, block] == me

            @pl.when(hit)
            def _():
                column_ref[place * cap + rank] = block

            rank = rank + jnp.where(hit, 1, 0)
        return 0

    lax.fori_loop(0, dp_count, source, 0)


def sort_kernel(cap, piece_count, dest_hbm, key_hbm, value_hbm, query_hbm, kv_hbm, same_hbm, other_hbm, *scratch):
    dest_ref, block_ref, count_ref, place_ref, key_ref, value_ref, query_ref, stage_ref, in_sem, out_sem = scratch
    arrivals = [
        pltpu.make_async_copy(source, target, in_sem.at[index])
        for index, (source, target) in enumerate(
            ((dest_hbm, dest_ref), (key_hbm, key_ref), (value_hbm, value_ref), (query_hbm, query_ref))
        )
    ]
    for arrival in arrivals:
        arrival.start()
    arrivals[0].wait()
    find_blocks(dest_ref, block_ref, place_ref, count_ref, cap)
    arrivals[1].wait()
    arrivals[2].wait()
    width = key_ref.shape[2]
    slot_count = kv_hbm.shape[0]
    for slot in range(slot_count):
        block = block_ref[slot]
        stage_ref[slot, :, :width] = key_ref[block]
        stage_ref[slot, :, width:] = value_ref[block]
    departures = [pltpu.make_async_copy(stage_ref, kv_hbm, out_sem.at[slot_count])]
    departures[0].start()
    arrivals[3].wait()
    for odd, out in ((1, other_hbm), (0, same_hbm)):
        for place in range(piece_count * cap):
            slot = (2 * (place // cap) + odd) * cap + place % cap
            departure = pltpu.make_async_copy(query_ref.at[place_ref[slot]], out.at[place], out_sem.at[slot])
            departure.start()
            departures.append(departure)
    for departure in departures:
        departure.wait()


def merge_query_kernel(cap, piece_count, same_ref, other_ref, *pieces):
    for piece in range(piece_count):
        rows = slice(piece * cap, (piece + 1) * cap)
        pieces[piece][:cap] = same_ref[rows]
        pieces[piece][cap:] = other_ref[rows]


def unsort_query_kernel(cap, piece_count, dest_ref, *rest):
    pieces = rest[:piece_count]
    out_ref, column_ref = rest[piece_count:]
    find_columns(dest_ref, column_ref, cap, True)
    for piece in range(piece_count):
        for place in range(2 * cap):
            out_ref[column_ref[2 * piece * cap + place]] = pieces[piece][place]


def unsort_kv_kernel(cap, dest_ref, bins_ref, seg_ref, got_ref, *rest):
    outs, (bin_ref, column_ref) = rest[:-2], rest[-2:]
    find_columns(dest_ref, column_ref, cap, False)
    lane = lax.broadcasted_iota(jnp.int32, (1, HD), 1)
    bins = jnp.zeros((1, HD), jnp.int32)
    for seg in range(SEGS):
        bins = jnp.where(lane == BIN_LANE + seg, bins_ref[0, seg], bins)
    bin_ref[...] = bins.astype(jnp.float32)
    block_count = got_ref.shape[0]
    for slot in range(block_count):
        column = column_ref[slot]
        first = 0
        for out_ref, groups in zip(outs, SHARES):
            width = groups * HD
            for half in range(2):
                start = half * HK * HD + first
                out_ref[column, :, half * width : (half + 1) * width] = got_ref[slot, :, start : start + width]
            first += width
    labels = seg_ref[...].astype(jnp.float32)
    labels = jnp.concatenate([labels] * (outs[0].shape[2] // labels.shape[1]), axis=1)
    outs[0][block_count] = jnp.broadcast_to(labels, outs[0].shape[1:]).astype(outs[0].dtype)


def after_kernel(*refs):
    pass


def rows_of(ref, block_count, lane):
    return ref[:block_count, :, lane : lane + HD].reshape(block_count * BLK, HD)


def allowed_bias(label_ref, hop, seg_row):
    row_count = seg_row.shape[1]
    square = (row_count, row_count)
    labels = label_ref[label_ref.shape[0] - 1][:1, :row_count].astype(jnp.float32)
    labels = jnp.transpose(jnp.broadcast_to(labels, square))
    allowed = labels == seg_row.astype(jnp.float32)
    if hop == 0:
        key_pos = lax.broadcasted_iota(jnp.int32, square, 0)
        query_pos = lax.broadcasted_iota(jnp.int32, square, 1)
        allowed = allowed & (key_pos <= query_pos)
    else:
        allowed = allowed & (lax.axis_index("ctx") >= hop)
    return jnp.where(allowed, 0.0, NEG)


def score(keys, query_ref, head):
    here = slice(head * HD, (head + 1) * HD)
    query = query_ref[:, :, here].reshape(query_ref.shape[0] * BLK, HD)
    return lax.dot_general(keys, query, (((1,), (1,)), ((), ())), preferred_element_type=jnp.float32)


def attend_share(share, query_ref, parts, out_ref, bias_ref):
    before = sum(SHARES[:share])
    held = [keys_and_values(share, index, query_ref.shape[0], parts) for index in range(SHARES[share])]
    heads = range(before * GROUP, (before + SHARES[share]) * GROUP)
    owners = [held[head // GROUP - before] for head in heads]
    scores = [score(keys, query_ref, head) for head, (keys, _) in zip(heads, owners)]
    mixed = attend_rows(scores, [values for _, values in owners], bias_ref[...])
    attended = [jnp.transpose(each) for each in mixed]
    for head, each in zip(heads, attended):
        first = (head - before * GROUP) * HD
        out_ref[:, first : first + HD] = each


def keys_and_values(share, index, block_count, parts):
    lane = index * HD
    keys = jnp.concatenate([rows_of(part, block_count, lane) for part in parts], axis=0)
    lane = (SHARES[share] + index) * HD
    values = jnp.concatenate([rows_of(part, block_count, lane) for part in parts], axis=0)
    return keys, jnp.transpose(values)


def attend_rows(scores, values, bias):
    scores = [each + bias for each in scores]
    tops = [jnp.max(each, axis=0, keepdims=True) for each in scores]
    weights = [jnp.exp2((each - top) * FACTOR) for each, top in zip(scores, tops)]
    totals = [jnp.sum(each, axis=0, keepdims=True) for each in weights]
    mixed = [
        jnp.dot(value, each.astype(jnp.bfloat16), preferred_element_type=jnp.float32)
        for value, each in zip(values, weights)
    ]
    return [(each * (1.0 / total)).astype(jnp.bfloat16) for each, total in zip(mixed, totals)]


def last_rows(seg_row):
    row_count = seg_row.shape[1]
    position = lax.broadcasted_iota(jnp.int32, (1, row_count), 1)
    after = jnp.concatenate([seg_row[:, 1:], seg_row[:, :1]], axis=1)
    is_last = (after != seg_row) | (position == row_count - 1)
    seg = lax.broadcasted_iota(jnp.int32, (GROUP * SEGS, row_count), 0) % SEGS
    return jnp.where((seg_row == seg) & is_last, 1.0, 0.0).astype(jnp.bfloat16)


def end_rewards(share, end_query_ref, end_bias_ref, end_weight_ref, parts, block_count):
    before = sum(SHARES[:share])
    groups = range(before, before + SHARES[share])
    held = [keys_and_values(share, group - before, block_count, parts) for group in groups]
    scores = [
        lax.dot_general(
            keys, end_query_ref[group], (((1,), (1,)), ((), ())), preferred_element_type=jnp.float32
        )
        for group, (keys, _) in zip(groups, held)
    ]
    attended = attend_rows(scores, [values for _, values in held], end_bias_ref[...])
    products = [each.astype(jnp.float32) * end_weight_ref[group] for group, each in zip(groups, attended)]
    return sum(jnp.sum(each, axis=0, keepdims=True) for each in products)


def first_kernel(seg_ref, weight_ref, query_ref, *rest):
    parts, rest = rest[:-6], rest[-6:]
    out_ref, bias_ref, end_query_ref, end_bias_ref, end_weight_ref, reward_ref = rest
    row_count = seg_ref.shape[1]
    block_count = query_ref.shape[0]
    for hop, part in enumerate(parts):
        bias_ref[hop * row_count : (hop + 1) * row_count, :] = allowed_bias(part, hop, seg_ref[...])
    chosen = last_rows(seg_ref[...])
    end_bias_ref[...] = lax.dot_general(
        bias_ref[...].astype(jnp.bfloat16),
        chosen,
        (((1,), (1,)), ((), ())),
        preferred_element_type=jnp.float32,
    )
    for group in range(HK):
        rows, weights = [], []
        for head in range(group * GROUP, (group + 1) * GROUP):
            here = slice(head * HD, (head + 1) * HD)
            query = query_ref[:, :, here].reshape(row_count, HD)
            rows.append(jnp.dot(chosen[:SEGS], query, preferred_element_type=jnp.float32))
            weights.append(jnp.broadcast_to(weight_ref[:, here], (SEGS, HD)))
        end_query_ref[group] = jnp.concatenate(rows, axis=0).astype(jnp.bfloat16)
        end_weight_ref[group] = jnp.transpose(jnp.concatenate(weights, axis=0))
    reward_ref[...] = end_rewards(0, end_query_ref, end_bias_ref, end_weight_ref, parts, block_count)
    attend_share(0, query_ref, parts, out_ref, bias_ref)


def ends_kernel(seg_ref, end_query_ref, end_bias_ref, end_weight_ref, reward_ref, bin_ref, *rest):
    parts, hist_ref = rest[:-1], rest[-1]
    seg_row = seg_ref[...]
    row_count = seg_row.shape[1]
    block_count = row_count // BLK
    reward = reward_ref[...] + end_rewards(
        1, end_query_ref, end_bias_ref, end_weight_ref, parts, block_count
    )
    by_seg = reward[:, :SEGS]
    for head in range(1, GROUP):
        by_seg = by_seg + reward[:, head * SEGS : (head + 1) * SEGS]
    by_seg = jnp.concatenate([by_seg, jnp.zeros((1, HD - SEGS), jnp.float32)], axis=1)
    lane = lax.broadcasted_iota(jnp.int32, (1, HD), 1)
    seg_rows = jnp.transpose(jnp.broadcast_to(seg_row, (row_count, row_count)))
    present = jnp.max(jnp.where(seg_rows == lane, 1, 0), axis=0, keepdims=True)
    first_seg, last_seg = seg_row[:, :1], seg_row[:, row_count - 1 :]
    row = bin_ref[...] + jnp.where(present > 0, by_seg, 0.0)
    row = row + jnp.where(lane == FIRST_LANE, first_seg.astype(jnp.float32), 0.0)
    row = row + jnp.where(lane == LAST_LANE, last_seg.astype(jnp.float32), 0.0)
    hist_ref[...] = jnp.broadcast_to(row.reshape(1, 1, HD), hist_ref.shape)


def last_kernel(query_ref, before_ref, bias_ref, *rest):
    attend_share(1, query_ref, rest[:-1], rest[-1], bias_ref)


def total_kernel(ctx_count, rows_ref, out_ref):
    device_count = rows_ref.shape[0]
    rows = rows_ref[...]
    first = rows[:, :, FIRST_LANE : FIRST_LANE + 1]
    last = rows[:, :, LAST_LANE : LAST_LANE + 1]
    following = jnp.concatenate([first[1:], first[:1]], axis=0)
    device = lax.broadcasted_iota(jnp.int32, first.shape, 0)
    ends = (following != last) | (lax.rem(device, ctx_count) == ctx_count - 1)
    lane = lax.broadcasted_iota(jnp.int32, rows.shape, 2)
    kept = (lane < SEGS) & ((lane.astype(jnp.float32) != last) | ends)
    rewards = jnp.where(kept, rows, 0.0)
    groups = (device_count // ctx_count, ctx_count, 1, HD)
    rewards = jnp.sum(rewards.reshape(groups), axis=1).reshape(groups[0], HD)
    bins = rows.reshape(groups)[:, 0].reshape(groups[0], HD)
    bin_id = lax.broadcasted_iota(jnp.int32, (groups[0], BINS), 1).astype(jnp.float32)
    hist = jnp.zeros((groups[0], BINS), jnp.float32)
    for seg in range(SEGS):
        bin_of = bins[:, BIN_LANE + seg : BIN_LANE + seg + 1]
        hist = hist + jnp.where(bin_id == bin_of, rewards[:, seg : seg + 1], 0.0)
    out_ref[...] = jnp.sum(hist, axis=0, keepdims=True)


def local(roll_query, roll_keys, roll_values, pack_dest, segment_ids, reward_bins, reward_weight):
    dp_count = lax.axis_size("dp")
    ctx_count = lax.axis_size("ctx")
    row_count = roll_query.shape[1]
    q_width = roll_query.shape[2]
    kv_width = roll_keys.shape[2]
    block_count = row_count // BLK
    cap = (block_count + dp_count - 1) // dp_count
    slot_count = dp_count * cap
    piece_count = dp_count // 2
    reach = row_count * ctx_count // 2
    hop_count = min(ctx_count - 1, (reach - 1 + row_count - 1) // row_count)
    device_count = dp_count * ctx_count
    smem = pl.BlockSpec(memory_space=pltpu.SMEM)
    vmem = pl.BlockSpec(memory_space=pltpu.VMEM)
    hbm = pl.BlockSpec(memory_space=pl.ANY)

    def across(array, distance):
        return lax.ppermute(array, "dp", [(i, i ^ distance) for i in range(dp_count)])

    half = jax.ShapeDtypeStruct((piece_count * cap, BLK, q_width), jnp.bfloat16)
    sorted_kv, same_query, other_query = pl.pallas_call(
        lambda *refs: sort_kernel(cap, piece_count, *refs),
        out_shape=[jax.ShapeDtypeStruct((slot_count, BLK, 2 * kv_width), jnp.bfloat16), half, half],
        in_specs=[hbm] * 4,
        out_specs=[hbm] * 3,
        scratch_shapes=[
            pltpu.SMEM((dp_count, block_count), jnp.int32),
            pltpu.SMEM((slot_count,), jnp.int32),
            pltpu.SMEM((dp_count,), jnp.int32),
            pltpu.SMEM((slot_count,), jnp.int32),
            pltpu.VMEM((block_count, BLK, kv_width), jnp.bfloat16),
            pltpu.VMEM((block_count, BLK, kv_width), jnp.bfloat16),
            pltpu.VMEM((block_count, BLK, q_width), jnp.bfloat16),
            pltpu.VMEM((slot_count, BLK, 2 * kv_width), jnp.bfloat16),
            pltpu.SemaphoreType.DMA((4,)),
            pltpu.SemaphoreType.DMA((slot_count + 1,)),
        ],
        compiler_params=params(60),
        name="sort",
    )(
        pack_dest,
        roll_keys.reshape(block_count, BLK, kv_width),
        roll_values.reshape(block_count, BLK, kv_width),
        roll_query.reshape(block_count, BLK, q_width),
    )
    got_kv = lax.all_to_all(
        sorted_kv.reshape(dp_count, cap * BLK, 2 * kv_width), "dp", split_axis=0, concat_axis=0, tiled=True
    ).reshape(slot_count, BLK, 2 * kv_width)

    pieces = pl.pallas_call(
        lambda *refs: merge_query_kernel(cap, piece_count, *refs),
        out_shape=[jax.ShapeDtypeStruct((2 * cap, BLK, q_width), jnp.bfloat16)] * piece_count,
        in_specs=[vmem] * 2,
        out_specs=[vmem] * piece_count,
        compiler_params=params(16),
        name="merge_query",
    )(same_query, across(other_query, 1))
    got_query = [pieces[0]] + [across(pieces[i], 2 * i) for i in range(1, piece_count)]
    query = pl.pallas_call(
        lambda *refs: unsort_query_kernel(cap, piece_count, *refs),
        out_shape=jax.ShapeDtypeStruct((block_count, BLK, q_width), jnp.bfloat16),
        in_specs=[smem] + [vmem] * piece_count,
        out_specs=vmem,
        scratch_shapes=[pltpu.SMEM((slot_count,), jnp.int32)],
        compiler_params=params(16),
        name="unsort_query",
    )(pack_dest, *got_query)

    *own, bin_of = pl.pallas_call(
        lambda *refs: unsort_kv_kernel(cap, *refs),
        out_shape=[
            jax.ShapeDtypeStruct((block_count + (share == 0), BLK, 2 * groups * HD), jnp.bfloat16)
            for share, groups in enumerate(SHARES)
        ]
        + [jax.ShapeDtypeStruct((1, HD), jnp.float32)],
        in_specs=[smem, smem, vmem, vmem],
        out_specs=[vmem] * (len(SHARES) + 1),
        scratch_shapes=[pltpu.SMEM((slot_count,), jnp.int32)],
        compiler_params=params(16),
        cost_estimate=cost(23000000000, 0),
        name="unsort_kv",
    )(pack_dest, reward_bins, segment_ids, got_kv)
    parts = [own]
    forward = [(i, i + 1) for i in range(ctx_count - 1)]
    for _ in range(hop_count):
        arrays = list(parts[-1])
        if len(parts) == hop_count:
            arrays[-1] = pl.pallas_call(
                after_kernel,
                out_shape=jax.ShapeDtypeStruct(arrays[-1].shape, arrays[-1].dtype),
                in_specs=[hbm] * 2,
                out_specs=hbm,
                input_output_aliases={0: 0},
                compiler_params=params(1),
                name="after_query",
            )(arrays[-1], query)
        parts.append([lax.ppermute(array, "ctx", forward) for array in arrays])

    weight_row = reward_weight.reshape(1, q_width)
    out_shape = jax.ShapeDtypeStruct((row_count, q_width), jnp.bfloat16)
    part_count = len(parts)
    first_width, last_width = (groups * GROUP * HD for groups in SHARES)
    ends = GROUP * SEGS
    attended, bias, *end_state = pl.pallas_call(
        first_kernel,
        grid=(1,),
        out_shape=(
            out_shape,
            jax.ShapeDtypeStruct((part_count * row_count, row_count), jnp.float32),
            jax.ShapeDtypeStruct((HK, ends, HD), jnp.bfloat16),
            jax.ShapeDtypeStruct((part_count * row_count, ends), jnp.float32),
            jax.ShapeDtypeStruct((HK, HD, ends), jnp.float32),
            jax.ShapeDtypeStruct((1, ends), jnp.float32),
        ),
        in_specs=[vmem] * (3 + part_count),
        out_specs=(pl.BlockSpec((row_count, first_width), lambda i: (0, 0)),) + (vmem,) * 5,
        compiler_params=params(16),
        name="first_share",
    )(segment_ids, weight_row, query, *[part[0] for part in parts])
    hist_rows = pl.pallas_call(
        ends_kernel,
        out_shape=jax.ShapeDtypeStruct((device_count, 1, HD), jnp.float32),
        in_specs=[vmem] * (6 + part_count),
        out_specs=vmem,
        compiler_params=params(16),
        name="ends",
    )(segment_ids, *end_state, bin_of, *[part[1] for part in parts])
    attended = pl.pallas_call(
        last_kernel,
        grid=(1,),
        out_shape=out_shape,
        in_specs=[vmem, hbm] + [vmem] * (1 + part_count),
        out_specs=pl.BlockSpec((row_count, last_width), lambda i: (0, first_width // last_width)),
        input_output_aliases={1: 0},
        compiler_params=params(16),
        name="last_share",
    )(query, attended, bias, *[part[1] for part in parts])
    gathered = lax.all_to_all(hist_rows, ("dp", "ctx"), split_axis=0, concat_axis=0, tiled=True)
    total = pl.pallas_call(
        lambda *refs: total_kernel(ctx_count, *refs),
        out_shape=jax.ShapeDtypeStruct((1, BINS), jnp.float32),
        in_specs=[vmem],
        out_specs=vmem,
        compiler_params=params(16),
        name="total",
    )(gathered)
    return attended.reshape(1, row_count, q_width), total.reshape(BINS)


def solution(mesh):
    in_specs = (
        P("dp", "ctx", None),
        P("dp", "ctx", None),
        P("dp", "ctx", None),
        P(None, "ctx"),
        P("dp", "ctx"),
        P("dp", None),
        P(),
    )
    out_specs = (P("dp", "ctx", None), P())
    return jax.shard_map(local, mesh=mesh, in_specs=in_specs, out_specs=out_specs, check_vma=False)
```
